32 devices in a mesh: tm: 4 (over z), atom: 2 (over x), chan: 4 (over y, core).
Axes of the slice: x: 2, y: 2, z: 4, core: 2. Of those that a mesh axis runs over, the one named last changes fastest.
Arguments:
- signal: bfloat16 [256, 4096], P('chan', 'tm'), may hold values from -6 to 6
- codes_init: float32 [128, 4096], P('atom', 'tm'), may hold values from -4 to 4
- atom_bank: bfloat16 [128, 256, 512], P('atom', 'chan'), may hold values from -0.015625 to 0.015625
- step_size: float32 [128], P('atom'), may hold values from 0.1 to 0.5
- threshold: float32 [128], P('atom'), may hold values from 0.3 to 3
Outputs:
- final_codes: float32 [128, 4096], P('atom', 'tm')
- residual: float32 [256, 4096], P('chan', 'tm')
The draws below stay inside these ranges and needn't reach their ends.
All inputs are finite; a program needn't handle non-finite values.
Results may differ from the reference program's by a relative error of at most 0.0025.
Values may be sent and summed in bfloat16 or wider, within the bound.
No kernel may reach another device: no remote copies, remote signals or barrier semaphores. Data moves between devices by JAX's collectives and lax.ppermute only.
A program may use at most 64 MiB of HBM per device.

```python
import math
import jax
import jax.numpy as jnp
from jax import lax

ATOMS = 128
CHANNELS = 256
TAPS = 512
ITERS = 2
SAMPLES = 4096


def block_levels(stream_key, extent, shards, least, top_value):
    gain, own = 1.0, jax.random.fold_in(stream_key, 6)
    for position, parts in shards:
        steps = jnp.exp(jax.random.uniform(jax.random.fold_in(own, position), (parts,), jnp.float32, least / len(shards), top_value / len(shards)))
        gain = gain * jnp.repeat(steps, extent[position] // parts).reshape([-1 if axis == position else 1 for axis in range(len(extent))])
    return gain


def normal_values(rng, shape, width, limit, split=(), held_as=jnp.bfloat16):
    loudness = block_levels(rng, shape, split, -0.22, 0.18) if split else 1.0
    array = jax.random.normal(rng, shape, jnp.float32) * width * loudness
    return jnp.minimum(jnp.maximum(array, -limit), limit).astype(held_as)


def setup_inputs(seed: int = 0) -> dict:
    splits = jax.random.split(jax.random.key(seed), 6)
    return {
        "signal": normal_values(splits[0], (CHANNELS, SAMPLES), 1.0, 6.0, ((0, 4), (1, 4))),
        "codes_init": normal_values(splits[1], (ATOMS, SAMPLES), 0.5, 4.0, ((0, 2), (1, 4)), jnp.float32),
        "atom_bank": normal_values(splits[2], (ATOMS, CHANNELS, TAPS), (CHANNELS * TAPS) ** -0.5, 0.015625, ((0, 2), (1, 4))),
        "step_size": jnp.clip(jnp.exp(math.log(0.5) - 1.609438 * jax.random.uniform(splits[3], (ATOMS,), jnp.float32) ** block_levels(splits[3], (ATOMS,), ((0, 2),), -0.2, 0.2)), 0.1, 0.5),
        "threshold": jnp.clip(jnp.exp(math.log(3.0) - 2.3025851 * jax.random.uniform(splits[4], (ATOMS,), jnp.float32) ** block_levels(splits[4], (ATOMS,), ((0, 2),), -0.2, 0.2)), 0.3, 3.0),
    }


def convolve(extended, kernel, spec):
    return lax.conv_general_dilated(extended[None], kernel, (1,), "VALID", dimension_numbers=("NCH", spec, "NCH"), precision=lax.Precision.HIGHEST)[0]


def shrink(current, gradient, step_size, threshold):
    moved = current - step_size[:, None] * gradient
    bound = (step_size * threshold)[:, None]
    return moved - jnp.clip(moved, -bound, bound)


def reference(signal, codes_init, atom_bank, step_size, threshold):
    kernel = atom_bank.astype(jnp.float32)
    flipped = kernel[:, :, ::-1]
    current = codes_init
    misfit = None
    for sweep_index in range(ITERS):
        lowered = current.astype(jnp.bfloat16).astype(jnp.float32)
        padded = jnp.pad(lowered, ((0, 0), (TAPS - 1, 0)))
        recon = convolve(padded, flipped, "IOH")
        misfit = recon - signal.astype(jnp.float32)
        rounded = misfit.astype(jnp.bfloat16)
        trailing = jnp.pad(rounded.astype(jnp.float32), ((0, 0), (0, TAPS - 1)))
        gradient = convolve(trailing, kernel, "OIH")
        current = shrink(current, gradient, step_size, threshold)
    return current, misfit
```

```python
import functools

import jax
import jax.numpy as jnp
from jax import lax
from jax.experimental import pallas as pl
from jax.experimental.pallas import tpu as pltpu
from jax.sharding import PartitionSpec as P

ITERS = 2
PHASES = 4
RUN = 16
GROUP = 8
LANES = 128
VMEM = 56 * 1024 * 1024


def to_blocks(value):
    rows, slab = value.shape
    parts = slab // (RUN * PHASES)
    return (
        value.reshape(rows, parts, RUN, PHASES)
        .transpose(2, 1, 3, 0)
        .reshape(RUN, parts, PHASES * rows)
    )


def from_blocks(value):
    run, parts, width = value.shape
    rows = width // PHASES
    return (
        value.reshape(run, parts, PHASES, rows)
        .transpose(3, 1, 0, 2)
        .reshape(rows, parts * run * PHASES)
    )


def bank_kernel(taps, rows, bank_ref, even_ref, odd_ref, flat):
    atoms, chans, _ = bank_ref.shape
    tiles = even_ref.shape[0]
    margin = 8
    step = min(256, taps)
    eye = (
        lax.broadcasted_iota(jnp.int32, (step, step), 0)
        == lax.broadcasted_iota(jnp.int32, (step, step), 1)
    ).astype(jnp.bfloat16)
    zeros = jnp.zeros((margin, LANES), jnp.float32)

    def turn(pair, carry):
        first = bank_ref[2 * pair]
        second = bank_ref[2 * pair + 1]
        doubled = jnp.concatenate([first, first, second, second], axis=0)
        for which in range(2):
            base = pl.multiple_of((2 * pair + which) * rows, 8)
            flat[pl.ds(base, margin), :] = zeros
            flat[pl.ds(base + margin + taps, margin), :] = zeros
        for part in range(taps // step):
            turned = lax.dot_general(
                eye,
                doubled[:, part * step : (part + 1) * step],
                (((1,), (1,)), ((), ())),
                preferred_element_type=jnp.float32,
            )
            for which in range(2):
                base = pl.multiple_of((2 * pair + which) * rows + margin + part * step, 8)
                flat[pl.ds(base, step), :] = turned[:, which * LANES : (which + 1) * LANES]
        return carry

    lax.fori_loop(0, atoms // 2, turn, 0)

    low = lax.broadcasted_iota(jnp.int32, (atoms, LANES), 1) < chans

    def tap(index):
        return flat[pl.ds(index + margin, atoms, stride=rows), :]

    def merge(turn_index, carry):
        for inner in range(4):
            tile = turn_index * 4 + inner
            middle = tap(2 * tile - 3)
            later = tap(2 * tile - 2)
            even_ref[tile] = jnp.where(low, carry, middle).astype(jnp.bfloat16)
            odd_ref[tile] = jnp.where(low, middle, later).astype(jnp.bfloat16)
            carry = later
        return carry

    lax.fori_loop(0, tiles // 4, merge, tap(-4))


def bank_tiles(atom_bank):
    atoms, chans, taps = atom_bank.shape
    tiles = taps // 2 + 4
    rows = taps + 16
    block = 16
    shape = jax.ShapeDtypeStruct((tiles, atoms, LANES), jnp.bfloat16)
    spec = pl.BlockSpec((tiles, block, LANES), lambda i: (0, i, 0))
    return pl.pallas_call(
        functools.partial(bank_kernel, taps, rows),
        grid=(atoms // block,),
        in_specs=[pl.BlockSpec((block, chans, taps), lambda i: (i, 0, 0))],
        out_specs=[spec, spec],
        out_shape=[shape, shape],
        scratch_shapes=[pltpu.VMEM((block * rows, LANES), jnp.float32)],
        compiler_params=pltpu.CompilerParams(vmem_limit_bytes=VMEM),
        name="bank_tiles",
    )(atom_bank)


def conv_kernel(transposed, steps, own_ref, halo_ref, even_hbm, odd_hbm, out_ref, even, odd, base, spread, total, sems):
    run, parts, width = own_ref.shape
    halo = halo_ref.shape[1]
    chunks = sems.shape[1]
    tiles = even.shape[0]
    size = tiles // chunks

    def copies(chunk):
        span = pl.ds(chunk * size, size)
        return [
            pltpu.make_async_copy(even_hbm.at[span], even.at[span], sems.at[0, chunk]),
            pltpu.make_async_copy(odd_hbm.at[span], odd.at[span], sems.at[1, chunk]),
        ]

    for chunk in range(chunks):
        for copy in copies(chunk):
            copy.start()

    own = own_ref[...].astype(jnp.float32)
    beside = halo_ref[...].astype(jnp.float32)
    if transposed:
        base[:, :parts] = own
        base[:, parts:] = beside
    else:
        base[:, :halo] = beside
        base[:, halo:] = own
    for shift in range(halo + 1):
        spread[shift * run : (shift + 1) * run] = base[:, shift : shift + parts].astype(jnp.bfloat16)

    total[...] = jnp.zeros_like(total)

    def block(step):
        def pair(ref, start):
            return jnp.concatenate([ref[start], ref[start + 1]], axis=1)

        return jnp.concatenate(
            [
                pair(even, 2 * step + 2),
                pair(odd, 2 * step + 1),
                pair(even, 2 * step + 1),
                pair(odd, 2 * step),
            ],
            axis=0,
        )

    def rows(step):
        start = step if transposed else halo * run - step
        return spread[pl.ds(start, run)].reshape(run * parts, width)

    def add(first, count):
        left = jnp.concatenate([rows(first + i) for i in range(count)], axis=1)
        if transposed:
            right = jnp.concatenate([block(first + i) for i in range(count)], axis=1)
            dims = (((1,), (1,)), ((), ()))
        else:
            right = jnp.concatenate([block(first + i) for i in range(count)], axis=0)
            dims = (((1,), (0,)), ((), ()))
        total[...] += lax.dot_general(left, right, dims, preferred_element_type=jnp.float32)

    turns = steps // GROUP
    share = -(-turns // chunks)
    for chunk in range(chunks):
        for copy in copies(chunk):
            copy.wait()
        low = min(chunk * share, turns)
        high = min((chunk + 1) * share, turns)
        high = high if chunk == chunks - 1 else min(high, ((chunk + 1) * size - 4) // 2 // GROUP)
        low = low if chunk == 0 else min(low, (chunk * size - 4) // 2 // GROUP)

        def loop(turn_index, carry):
            add(turn_index * GROUP, GROUP)
            return carry

        lax.fori_loop(low, high, loop, 0)
    add(turns * GROUP, steps - turns * GROUP)
    out_ref[...] = total[...].reshape(out_ref.shape)


def convolve(own, halo, even, odd, transposed):
    run, parts, width = own.shape
    beside = halo.shape[1]
    tiles, atoms, _ = even.shape
    steps = (tiles - 4) // 2 + 1
    chunks = 4
    out_width = 2 * LANES if not transposed else PHASES * atoms
    flops = 2 * run * parts * width * out_width * steps
    return pl.pallas_call(
        functools.partial(conv_kernel, transposed, steps),
        in_specs=[
            pl.BlockSpec(memory_space=pltpu.VMEM),
            pl.BlockSpec(memory_space=pltpu.VMEM),
            pl.BlockSpec(memory_space=pl.ANY),
            pl.BlockSpec(memory_space=pl.ANY),
        ],
        out_specs=pl.BlockSpec(memory_space=pltpu.VMEM),
        out_shape=jax.ShapeDtypeStruct((run, parts, out_width), jnp.float32),
        scratch_shapes=[
            pltpu.VMEM(even.shape, jnp.bfloat16),
            pltpu.VMEM(odd.shape, jnp.bfloat16),
            pltpu.VMEM((run, parts + beside, width), jnp.float32),
            pltpu.VMEM(((beside + 1) * run, parts, width), jnp.bfloat16),
            pltpu.VMEM((run * parts, out_width), jnp.float32),
            pltpu.SemaphoreType.DMA((2, chunks)),
        ],
        compiler_params=pltpu.CompilerParams(vmem_limit_bytes=VMEM),
        cost_estimate=pl.CostEstimate(
            flops=flops, bytes_accessed=even.size * 4 + own.size * 8, transcendentals=0
        ),
        name="correlate" if transposed else "synthesize",
    )(own, halo, even, odd)


def shifted(value, axis, steps):
    count = lax.axis_size(axis)
    first, last = max(0, -steps), min(count, count - steps)
    return lax.ppermute(value, axis, [(i, i + steps) for i in range(first, last)])


def summed(value, axis):
    count = lax.axis_size(axis)
    step = 1
    while step < count:
        value = value + lax.ppermute(value, axis, [(i, i ^ step) for i in range(count)])
        step *= 2
    return value


def body(signal, codes_init, atom_bank, step_size, threshold):
    atoms, chans, taps = atom_bank.shape
    held = LANES // 2
    if chans < held:
        atom_bank = jnp.pad(atom_bank, ((0, 0), (0, held - chans), (0, 0)))
        signal = jnp.pad(signal, ((0, held - chans), (0, 0)))
    even, odd = bank_tiles(atom_bank)
    beside = taps // (RUN * PHASES)
    recorded = to_blocks(signal)
    current = to_blocks(codes_init)
    step = jnp.tile(step_size, PHASES)
    bound = jnp.tile(step_size * threshold, PHASES)
    for _ in range(ITERS):
        lowered = current.astype(jnp.bfloat16)
        earlier = shifted(lowered[:, -beside:], "tm", 1)
        recon = summed(convolve(lowered, earlier, even, odd, False), "atom")
        misfit = recon - recorded.astype(jnp.float32)
        rounded = misfit.astype(jnp.bfloat16)
        following = shifted(rounded[:, :beside], "tm", -1)
        gradient = summed(convolve(rounded, following, even, odd, True), "chan")
        moved = current - step * gradient
        current = moved - jnp.clip(moved, -bound, bound)
    return from_blocks(current), from_blocks(misfit)[:chans]


def solution(mesh):
    placed = (P("chan", "tm"), P("atom", "tm"), P("atom", "chan", None), P("atom"), P("atom"))
    return jax.shard_map(
        body,
        mesh=mesh,
        in_specs=placed,
        out_specs=(P("atom", "tm"), P("chan", "tm")),
        check_vma=False,
    )
```

```python
import functools

import jax
import jax.numpy as jnp
from jax import lax
from jax.experimental import pallas as pl
from jax.experimental.pallas import tpu as pltpu
from jax.sharding import PartitionSpec as P

ITERS = 2
PHASES = 4
RUN = 16
GROUP = 8
LANES = 128
VMEM = 24 * 1024 * 1024


def to_blocks(value):
    rows, slab = value.shape
    parts = slab // (RUN * PHASES)
    return (
        value.reshape(rows, parts, RUN, PHASES)
        .transpose(2, 1, 3, 0)
        .reshape(RUN, parts, PHASES * rows)
    )


def from_blocks(value):
    run, parts, width = value.shape
    rows = width // PHASES
    return (
        value.reshape(run, parts, PHASES, rows)
        .transpose(3, 1, 0, 2)
        .reshape(rows, parts * run * PHASES)
    )


def bank_kernel(taps, rows, low_ref, high_ref, even_ref, odd_ref, flat):
    atoms, chans, _ = low_ref.shape
    tiles = even_ref.shape[0]
    margin = 8
    step = min(256, taps)
    eye = (
        lax.broadcasted_iota(jnp.int32, (step, step), 0)
        == lax.broadcasted_iota(jnp.int32, (step, step), 1)
    ).astype(jnp.bfloat16)
    zeros = jnp.zeros((margin, LANES), jnp.float32)

    def turn(pair, carry):
        first, second = 2 * pair, 2 * pair + 1
        stacked = jnp.concatenate(
            [low_ref[first], high_ref[first], low_ref[second], high_ref[second]], axis=0
        )
        for which in range(2):
            base = (2 * pair + which) * rows
            flat[pl.ds(base, margin), :] = zeros
            flat[pl.ds(base + margin + taps, margin), :] = zeros
        for part in range(taps // step):
            turned = lax.dot_general(
                eye,
                stacked[:, part * step : (part + 1) * step],
                (((1,), (1,)), ((), ())),
                preferred_element_type=jnp.float32,
            )
            for which in range(2):
                base = (2 * pair + which) * rows + margin + part * step
                flat[pl.ds(base, step), :] = turned[:, which * LANES : (which + 1) * LANES]
        return carry

    lax.fori_loop(0, atoms // 2, turn, 0)

    low = lax.broadcasted_iota(jnp.int32, (atoms, LANES), 1) < chans

    def tap(index):
        value = flat[pl.ds(index + margin, atoms, stride=rows), :]
        return value, pltpu.roll(value, chans, 1)

    def store(ref, tile, early, late):
        ref[tile, 0] = jnp.where(low, early[0], late[1]).astype(jnp.bfloat16)
        ref[tile, 1] = jnp.where(low, early[1], late[0]).astype(jnp.bfloat16)

    def merge(turn_index, carry):
        for inner in range(4):
            tile = turn_index * 4 + inner
            middle = tap(2 * tile - 3)
            later = tap(2 * tile - 2)
            store(even_ref, tile, carry, middle)
            store(odd_ref, tile, middle, later)
            carry = later
        return carry

    lax.fori_loop(0, tiles // 4, merge, tap(-4))


def bank_tiles(atom_bank):
    atoms, chans, taps = atom_bank.shape
    tiles = taps // 2 + 4
    rows = taps + 17
    block = 16
    half = atoms // 2
    turns = half // block
    shape = jax.ShapeDtypeStruct((tiles, 2, half, LANES), jnp.bfloat16)
    spec = pl.BlockSpec((tiles, 2, block, LANES), lambda i: (0, 0, i, 0))
    even, odd = pl.pallas_call(
        functools.partial(bank_kernel, taps, rows),
        grid=(turns,),
        in_specs=[
            pl.BlockSpec((block, chans, taps), lambda i: (i, 0, 0)),
            pl.BlockSpec((block, chans, taps), lambda i: (i + turns, 0, 0)),
        ],
        out_specs=[spec, spec],
        out_shape=[shape, shape],
        scratch_shapes=[pltpu.VMEM((block * rows, LANES), jnp.float32)],
        compiler_params=pltpu.CompilerParams(vmem_limit_bytes=VMEM),
        name="bank_tiles",
    )(atom_bank, atom_bank)
    return even.reshape(tiles, atoms, LANES), odd.reshape(tiles, atoms, LANES)


def conv_kernel(transposed, steps, own_ref, halo_ref, even_hbm, odd_hbm, out_ref, even, odd, base, spread, total, sems):
    run, parts, width = own_ref.shape
    halo = halo_ref.shape[1]
    chunks = sems.shape[1]
    tiles = even.shape[0]
    size = tiles // chunks

    def copies(chunk):
        span = pl.ds(chunk * size, size)
        return [
            pltpu.make_async_copy(even_hbm.at[span], even.at[span], sems.at[0, chunk]),
            pltpu.make_async_copy(odd_hbm.at[span], odd.at[span], sems.at[1, chunk]),
        ]

    for chunk in range(chunks):
        for copy in copies(chunk):
            copy.start()

    own = own_ref[...].astype(jnp.float32)
    beside = halo_ref[...].astype(jnp.float32)
    if transposed:
        base[:, :parts] = own
        base[:, parts:] = beside
    else:
        base[:, :halo] = beside
        base[:, halo:] = own
    for shift in range(halo + 1):
        spread[shift * run : (shift + 1) * run] = base[:, shift : shift + parts].astype(jnp.bfloat16)

    total[...] = jnp.zeros_like(total)

    def block(step):
        def pair(ref, start):
            return jnp.concatenate([ref[start], ref[start + 1]], axis=1)

        return jnp.concatenate(
            [
                pair(even, 2 * step + 2),
                pair(odd, 2 * step + 1),
                pair(even, 2 * step + 1),
                pair(odd, 2 * step),
            ],
            axis=0,
        )

    def rows(step):
        start = step if transposed else halo * run - step
        return spread[pl.ds(start, run)].reshape(run * parts, width)

    def add(which, first, count):
        left = jnp.concatenate([rows(first + i) for i in range(count)], axis=1)
        if transposed:
            right = jnp.concatenate([block(first + i) for i in range(count)], axis=1)
            dims = (((1,), (1,)), ((), ()))
        else:
            right = jnp.concatenate([block(first + i) for i in range(count)], axis=0)
            dims = (((1,), (0,)), ((), ()))
        total[which] += lax.dot_general(left, right, dims, preferred_element_type=jnp.float32)

    turns = steps // GROUP
    share = -(-turns // chunks)
    for chunk in range(chunks):
        for copy in copies(chunk):
            copy.wait()
        low = min(chunk * share, turns)
        high = min((chunk + 1) * share, turns)
        high = high if chunk == chunks - 1 else min(high, ((chunk + 1) * size - 4) // 2 // GROUP)
        low = low if chunk == 0 else min(low, (chunk * size - 4) // 2 // GROUP)

        def loop(turn_index, carry):
            add(0, turn_index * GROUP, GROUP // 2)
            add(1, turn_index * GROUP + GROUP // 2, GROUP // 2)
            return carry

        lax.fori_loop(low, high, loop, 0)
    add(0, turns * GROUP, steps - turns * GROUP)
    out_ref[...] = (total[0] + total[1]).reshape(out_ref.shape).astype(out_ref.dtype)


def convolve(own, halo, even, odd, transposed):
    run, parts, width = own.shape
    beside = halo.shape[1]
    tiles, atoms, _ = even.shape
    steps = (tiles - 4) // 2 + 1
    chunks = 4
    out_width = 2 * LANES if not transposed else PHASES * atoms
    flops = 2 * run * parts * width * out_width * steps
    return pl.pallas_call(
        functools.partial(conv_kernel, transposed, steps),
        in_specs=[
            pl.BlockSpec(memory_space=pltpu.VMEM),
            pl.BlockSpec(memory_space=pltpu.VMEM),
            pl.BlockSpec(memory_space=pl.ANY),
            pl.BlockSpec(memory_space=pl.ANY),
        ],
        out_specs=pl.BlockSpec(memory_space=pltpu.VMEM),
        out_shape=jax.ShapeDtypeStruct(
            (run, parts, out_width), jnp.float32 if transposed else jnp.bfloat16
        ),
        scratch_shapes=[
            pltpu.VMEM(even.shape, jnp.bfloat16),
            pltpu.VMEM(odd.shape, jnp.bfloat16),
            pltpu.VMEM((run, parts + beside, width), jnp.float32),
            pltpu.VMEM(((beside + 1) * run, parts, width), jnp.bfloat16),
            pltpu.VMEM((2, run * parts, out_width), jnp.float32),
            pltpu.SemaphoreType.DMA((2, chunks)),
        ],
        compiler_params=pltpu.CompilerParams(vmem_limit_bytes=VMEM),
        cost_estimate=pl.CostEstimate(
            flops=flops, bytes_accessed=even.size * 4 + own.size * 8, transcendentals=0
        ),
        name="correlate" if transposed else "synthesize",
    )(own, halo, even, odd)


def shifted(value, axis, steps):
    count = lax.axis_size(axis)
    first, last = max(0, -steps), min(count, count - steps)
    return lax.ppermute(value, axis, [(i, i + steps) for i in range(first, last)])


def summed(value, axis):
    count = lax.axis_size(axis)
    step = 1
    while step < count:
        other = lax.ppermute(value, axis, [(i, i ^ step) for i in range(count)])
        value = value.astype(jnp.float32) + other.astype(jnp.float32)
        step *= 2
    return value


def body(signal, codes_init, atom_bank, step_size, threshold):
    atoms, chans, taps = atom_bank.shape
    held = LANES // 2
    if chans < held:
        atom_bank = jnp.pad(atom_bank, ((0, 0), (0, held - chans), (0, 0)))
        signal = jnp.pad(signal, ((0, held - chans), (0, 0)))
    even, odd = bank_tiles(atom_bank)
    beside = taps // (RUN * PHASES)
    recorded = to_blocks(signal)
    current = to_blocks(codes_init)
    step = jnp.tile(step_size, PHASES)
    bound = jnp.tile(step_size * threshold, PHASES)
    for _ in range(ITERS):
        lowered = current.astype(jnp.bfloat16)
        earlier = shifted(lowered[:, -beside:], "tm", 1)
        recon = summed(convolve(lowered, earlier, even, odd, False), "atom")
        misfit = recon - recorded.astype(jnp.float32)
        rounded = misfit.astype(jnp.bfloat16)
        following = shifted(rounded[:, :beside], "tm", -1)
        gradient = summed(convolve(rounded, following, even, odd, True), "chan")
        moved = current - step * gradient
        current = moved - jnp.clip(moved, -bound, bound)
    return from_blocks(current), from_blocks(misfit)[:chans]


def solution(mesh):
    placed = (P("chan", "tm"), P("atom", "tm"), P("atom", "chan", None), P("atom"), P("atom"))
    return jax.shard_map(
        body,
        mesh=mesh,
        in_specs=placed,
        out_specs=(P("atom", "tm"), P("chan", "tm")),
        check_vma=False,
    )
```

```python
import functools

import jax
import jax.numpy as jnp
from jax import lax
from jax.experimental import pallas as pl
from jax.experimental.pallas import tpu as pltpu
from jax.sharding import PartitionSpec as P

ITERS = 2
PHASES = 4
RUN = 16
LANES = 128
VMEM = 24 * 1024 * 1024


def to_blocks(value):
    rows, slab = value.shape
    parts = slab // (RUN * PHASES)
    return (
        value.reshape(rows, parts, RUN, PHASES)
        .transpose(2, 1, 3, 0)
        .reshape(RUN, parts, PHASES * rows)
    )


def from_blocks(value):
    run, parts, width = value.shape
    rows = width // PHASES
    return (
        value.reshape(run, parts, PHASES, rows)
        .transpose(3, 1, 0, 2)
        .reshape(rows, parts * run * PHASES)
    )


def bank_kernel(rows, bank_hbm, even_ref, odd_ref, bank, flat, sems):
    atoms, chans, taps = bank.shape
    tiles = even_ref.shape[0]
    half, turns = atoms // 2, sems.shape[0]
    block = half // turns
    margin = 8
    step = min(256, taps)
    eye = (
        lax.broadcasted_iota(jnp.int32, (step, step), 0)
        == lax.broadcasted_iota(jnp.int32, (step, step), 1)
    ).astype(jnp.bfloat16)
    zeros = jnp.zeros((margin, LANES), jnp.float32)
    low = lax.broadcasted_iota(jnp.int32, (block, LANES), 1) < chans

    copies = [
        [
            pltpu.make_async_copy(bank_hbm.at[span], bank.at[span], sems.at[group, which])
            for which, span in enumerate(
                (pl.ds(group * block, block), pl.ds(half + group * block, block))
            )
        ]
        for group in range(turns)
    ]
    for pair in copies:
        for copy in pair:
            copy.start()

    def tap(index):
        value = flat[pl.ds(index + margin, block, stride=rows), :]
        return value, pltpu.roll(value, chans, 1)

    for group in range(turns):
        for copy in copies[group]:
            copy.wait()

        def turn(pair, carry):
            first = group * block + 2 * pair
            stacked = jnp.concatenate(
                [bank[first], bank[half + first], bank[first + 1], bank[half + first + 1]], axis=0
            )
            for which in range(2):
                base = (2 * pair + which) * rows
                flat[pl.ds(base, margin), :] = zeros
                flat[pl.ds(base + margin + taps, margin), :] = zeros
            for part in range(taps // step):
                turned = lax.dot_general(
                    eye,
                    stacked[:, part * step : (part + 1) * step],
                    (((1,), (1,)), ((), ())),
                    preferred_element_type=jnp.float32,
                )
                for which in range(2):
                    base = (2 * pair + which) * rows + margin + part * step
                    flat[pl.ds(base, step), :] = turned[:, which * LANES : (which + 1) * LANES]
            return carry

        lax.fori_loop(0, block // 2, turn, 0)

        def store(ref, tile, early, late):
            start = group * block
            ref[tile, start : start + block] = jnp.where(low, early[0], late[1]).astype(jnp.bfloat16)
            start += half
            ref[tile, start : start + block] = jnp.where(low, early[1], late[0]).astype(jnp.bfloat16)

        unroll = next(n for n in (20, 13, 8, 5, 4, 2, 1) if tiles % n == 0)

        def merge(turn_index, carry):
            for inner in range(unroll):
                tile = turn_index * unroll + inner
                middle = tap(2 * tile - 3)
                later = tap(2 * tile - 2)
                store(even_ref, tile, carry, middle)
                store(odd_ref, tile, middle, later)
                carry = later
            return carry

        lax.fori_loop(0, tiles // unroll, merge, tap(-4))


def bank_tiles(atom_bank):
    atoms, chans, taps = atom_bank.shape
    tiles = taps // 2 + 4
    rows = taps + 17
    block = 16
    turns = atoms // 2 // block
    shape = jax.ShapeDtypeStruct((tiles, atoms, LANES), jnp.bfloat16)
    spec = pl.BlockSpec(memory_space=pltpu.VMEM)
    return pl.pallas_call(
        functools.partial(bank_kernel, rows),
        in_specs=[pl.BlockSpec(memory_space=pl.ANY)],
        out_specs=[spec, spec],
        out_shape=[shape, shape],
        scratch_shapes=[
            pltpu.VMEM(atom_bank.shape, jnp.bfloat16),
            pltpu.VMEM((block * rows, LANES), jnp.float32),
            pltpu.SemaphoreType.DMA((turns, 2)),
        ],
        compiler_params=pltpu.CompilerParams(vmem_limit_bytes=24 * 1024 * 1024),
        name="bank_tiles",
    )(atom_bank)


def conv_kernel(transposed, steps, group, split, own_ref, halo_ref, even, odd, out_ref, base, spread, total):
    run, parts, width = own_ref.shape
    halo = halo_ref.shape[1]
    lanes = width // LANES

    own = own_ref[...].astype(jnp.float32)
    beside = halo_ref[...].astype(jnp.float32)
    if transposed:
        base[:, :parts] = own
        base[:, parts:] = beside
    else:
        base[:, :halo] = beside
        base[:, halo:] = own
    for shift in range(halo + 1):
        window = base[:, shift : shift + parts].astype(jnp.bfloat16)
        for lane in range(lanes):
            spread[lane, shift * run : (shift + 1) * run] = window[:, :, lane * LANES : (lane + 1) * LANES]

    total[...] = jnp.zeros_like(total)

    def block(step):
        def pair(ref, start):
            return jnp.concatenate([ref[start], ref[start + 1]], axis=1)

        return jnp.concatenate(
            [
                pair(even, 2 * step + 2),
                pair(odd, 2 * step + 1),
                pair(even, 2 * step + 1),
                pair(odd, 2 * step),
            ],
            axis=0,
        )

    def rows(step):
        start = step if transposed else halo * run - step
        return [
            spread[lane, pl.ds(start, run)].reshape(run * parts, LANES) for lane in range(lanes)
        ]

    def add(which, first, count):
        left = jnp.concatenate([part for i in range(count) for part in rows(first + i)], axis=1)
        if transposed:
            right = jnp.concatenate([block(first + i) for i in range(count)], axis=1)
            dims = (((1,), (1,)), ((), ()))
        else:
            right = jnp.concatenate([block(first + i) for i in range(count)], axis=0)
            dims = (((1,), (0,)), ((), ()))
        total[which] += lax.dot_general(left, right, dims, preferred_element_type=jnp.float32)

    cuts = [group * i // split for i in range(split + 1)]

    def loop(turn_index, carry):
        for i in range(split):
            add(i, turn_index * group + cuts[i], cuts[i + 1] - cuts[i])
        return carry

    turns = steps // group
    lax.fori_loop(0, turns, loop, 0)
    if steps > turns * group:
        add(0, turns * group, steps - turns * group)
    result = total[0]
    for i in range(1, split):
        result = result + total[i]
    out_ref[...] = result.reshape(out_ref.shape).astype(out_ref.dtype)


def convolve(own, halo, even, odd, transposed, group, split):
    run, parts, width = own.shape
    beside = halo.shape[1]
    tiles, atoms, _ = even.shape
    steps = (tiles - 4) // 2 + 1
    out_width = 2 * LANES if not transposed else PHASES * atoms
    flops = 2 * run * parts * width * out_width * steps
    return pl.pallas_call(
        functools.partial(conv_kernel, transposed, steps, group, split),
        in_specs=[pl.BlockSpec(memory_space=pltpu.VMEM)] * 4,
        out_specs=pl.BlockSpec(memory_space=pltpu.VMEM),
        out_shape=jax.ShapeDtypeStruct(
            (run, parts, out_width), jnp.float32 if transposed else jnp.bfloat16
        ),
        scratch_shapes=[
            pltpu.VMEM((run, parts + beside, width), jnp.float32),
            pltpu.VMEM((width // LANES, (beside + 1) * run, parts, LANES), jnp.bfloat16),
            pltpu.VMEM((split, run * parts, out_width), jnp.float32),
        ],
        compiler_params=pltpu.CompilerParams(vmem_limit_bytes=VMEM),
        cost_estimate=pl.CostEstimate(
            flops=flops, bytes_accessed=even.size * 4 + own.size * 8, transcendentals=0
        ),
        name="correlate" if transposed else "synthesize",
    )(own, halo, even, odd)


def shifted(value, axis, steps):
    count = lax.axis_size(axis)
    first, last = max(0, -steps), min(count, count - steps)
    return lax.ppermute(value, axis, [(i, i + steps) for i in range(first, last)])


def summed(value, axis):
    count = lax.axis_size(axis)
    step = 1
    while step < count:
        if step > 1:
            value = value.astype(jnp.bfloat16)
        other = lax.ppermute(value, axis, [(i, i ^ step) for i in range(count)])
        value = value.astype(jnp.float32) + other.astype(jnp.float32)
        step *= 2
    return value


def body(signal, codes_init, atom_bank, step_size, threshold):
    atoms, chans, taps = atom_bank.shape
    held = LANES // 2
    if chans < held:
        atom_bank = jnp.pad(atom_bank, ((0, 0), (0, held - chans), (0, 0)))
        signal = jnp.pad(signal, ((0, held - chans), (0, 0)))
    even, odd = bank_tiles(atom_bank)
    beside = taps // (RUN * PHASES)
    recorded = to_blocks(signal)
    current = to_blocks(codes_init)
    step = jnp.tile(step_size, PHASES)
    bound = jnp.tile(step_size * threshold, PHASES)
    for sweep in range(ITERS):
        shape = (16, 2) if sweep == 0 else (43, 2)
        lowered = current.astype(jnp.bfloat16)
        earlier = shifted(lowered[:, -beside:], "tm", 1)
        recon = summed(convolve(lowered, earlier, even, odd, False, *shape), "atom")
        misfit = recon - recorded.astype(jnp.float32)
        rounded = misfit.astype(jnp.bfloat16)
        following = shifted(rounded[:, :beside], "tm", -1)
        gradient = summed(convolve(rounded, following, even, odd, True, *shape), "chan")
        moved = current - step * gradient
        current = moved - jnp.clip(moved, -bound, bound)
    return from_blocks(current), from_blocks(misfit)[:chans]


def solution(mesh):
    placed = (P("chan", "tm"), P("atom", "tm"), P("atom", "chan", None), P("atom"), P("atom"))
    return jax.shard_map(
        body,
        mesh=mesh,
        in_specs=placed,
        out_specs=(P("atom", "tm"), P("chan", "tm")),
        check_vma=False,
    )
```

```python
import functools

import jax
import jax.numpy as jnp
from jax import lax
from jax.experimental import pallas as pl
from jax.experimental.pallas import tpu as pltpu
from jax.sharding import PartitionSpec as P

ITERS = 2
PHASES = 4
PARTS = 16
LANES = 128
VMEM = 24 * 1024 * 1024


def blocks_kernel(count, *refs):
    values, outs, flat = refs[:count], refs[count:-1], refs[-1]
    for index, value_ref in enumerate(values):
        halves = outs[2 * index : 2 * index + 2]
        rows, slab = value_ref.shape
        run, parts, _ = halves[0].shape
        length = run * PHASES
        pitch = length + 1
        value = value_ref[...].astype(jnp.float32)
        turned = jnp.concatenate([value, value], axis=0).T
        for part in range(slab // length):
            flat[part * pitch : part * pitch + length] = turned[part * length : (part + 1) * length]
        low = lax.broadcasted_iota(jnp.int32, (parts, LANES), 1) < rows
        for half, out in enumerate(halves):
            for q in range(run):
                first = half * parts * pitch + q * PHASES
                phases = [flat[pl.ds(first + s, parts, stride=pitch), :] for s in range(PHASES)]
                out[q] = jnp.concatenate(
                    [jnp.where(low, phases[s], phases[s + 1]) for s in range(0, PHASES, 2)], axis=1
                )


def to_blocks(taps, *values):
    run = taps // (PHASES * PARTS)
    half = jax.ShapeDtypeStruct((run, PARTS, PHASES * LANES // 2), jnp.float32)
    slab = values[0].shape[1]
    return pl.pallas_call(
        functools.partial(blocks_kernel, len(values)),
        in_specs=[pl.BlockSpec(memory_space=pltpu.VMEM)] * len(values),
        out_specs=[pl.BlockSpec(memory_space=pltpu.VMEM)] * (2 * len(values)),
        out_shape=[half] * (2 * len(values)),
        scratch_shapes=[pltpu.VMEM((slab + slab // (run * PHASES) + 7, LANES), jnp.float32)],
        compiler_params=pltpu.CompilerParams(vmem_limit_bytes=VMEM),
        name="to_blocks",
    )(*values)


def series_kernel(low_ref, high_ref, out_ref, flat):
    rows, slab = out_ref.shape
    run, parts, _ = low_ref.shape
    length = run * PHASES
    pitch = length + 1
    for half, value_ref in enumerate((low_ref, high_ref)):
        for q in range(run):
            first = half * parts * pitch + q * PHASES
            for s in range(0, PHASES, 2):
                pair = value_ref[q, :, s // 2 * LANES : (s // 2 + 1) * LANES]
                flat[pl.ds(first + s, parts, stride=pitch), :] = pair
                flat[pl.ds(first + s + 1, parts, stride=pitch), :] = pltpu.roll(pair, LANES // 2, 1)
    turned = jnp.concatenate(
        [flat[part * pitch : part * pitch + length] for part in range(slab // length)], axis=0
    ).T
    out_ref[...] = turned[:rows]


def from_blocks(low, high):
    run, parts, width = low.shape
    slab = 2 * run * parts * PHASES
    return pl.pallas_call(
        series_kernel,
        in_specs=[pl.BlockSpec(memory_space=pltpu.VMEM)] * 2,
        out_specs=pl.BlockSpec(memory_space=pltpu.VMEM),
        out_shape=jax.ShapeDtypeStruct((width // PHASES, slab), jnp.float32),
        scratch_shapes=[pltpu.VMEM((slab + slab // (run * PHASES) + 7, LANES), jnp.float32)],
        compiler_params=pltpu.CompilerParams(vmem_limit_bytes=VMEM),
        name="from_blocks",
    )(low, high)


def bank_kernel(rows, bank_hbm, even_ref, odd_ref, bank, flat, sems):
    atoms, chans, taps = bank.shape
    tiles = even_ref.shape[0]
    half, turns = atoms // 2, sems.shape[0]
    block = half // turns
    margin = 8
    step = min(256, taps)
    eye = (
        lax.broadcasted_iota(jnp.int32, (step, step), 0)
        == lax.broadcasted_iota(jnp.int32, (step, step), 1)
    ).astype(jnp.bfloat16)
    zeros = jnp.zeros((margin, LANES), jnp.float32)
    low = lax.broadcasted_iota(jnp.int32, (block, LANES), 1) < chans

    copies = [
        [
            pltpu.make_async_copy(bank_hbm.at[span], bank.at[span], sems.at[group, which])
            for which, span in enumerate(
                (pl.ds(group * block, block), pl.ds(half + group * block, block))
            )
        ]
        for group in range(turns)
    ]
    for pair in copies:
        for copy in pair:
            copy.start()

    def tap(index):
        value = flat[pl.ds(index + margin, block, stride=rows), :]
        return value, pltpu.roll(value, chans, 1)

    for group in range(turns):
        for copy in copies[group]:
            copy.wait()

        def turn(pair, carry):
            first = group * block + 2 * pair
            stacked = jnp.concatenate(
                [bank[first], bank[half + first], bank[first + 1], bank[half + first + 1]], axis=0
            )
            for which in range(2):
                base = (2 * pair + which) * rows
                flat[pl.ds(base, margin), :] = zeros
                flat[pl.ds(base + margin + taps, margin), :] = zeros
            for part in range(taps // step):
                turned = lax.dot_general(
                    eye,
                    stacked[:, part * step : (part + 1) * step],
                    (((1,), (1,)), ((), ())),
                    preferred_element_type=jnp.float32,
                )
                for which in range(2):
                    base = (2 * pair + which) * rows + margin + part * step
                    flat[pl.ds(base, step), :] = turned[:, which * LANES : (which + 1) * LANES]
            return carry

        lax.fori_loop(0, block // 2, turn, 0)

        def store(ref, tile, early, late):
            start = group * block
            ref[tile, start : start + block] = jnp.where(low, early[0], late[1]).astype(jnp.bfloat16)
            start += half
            ref[tile, start : start + block] = jnp.where(low, early[1], late[0]).astype(jnp.bfloat16)

        unroll = next(n for n in (20, 13, 8, 5, 4, 2, 1) if tiles % n == 0)

        def merge(turn_index, carry):
            for inner in range(unroll):
                tile = turn_index * unroll + inner
                middle = tap(2 * tile - 3)
                later = tap(2 * tile - 2)
                store(even_ref, tile, carry, middle)
                store(odd_ref, tile, middle, later)
                carry = later
            return carry

        lax.fori_loop(0, tiles // unroll, merge, tap(-4))


def bank_tiles(atom_bank):
    atoms, chans, taps = atom_bank.shape
    tiles = taps // 2 + 4
    rows = taps + 17
    block = 16
    turns = atoms // 2 // block
    shape = jax.ShapeDtypeStruct((tiles, atoms, LANES), jnp.bfloat16)
    spec = pl.BlockSpec(memory_space=pltpu.VMEM)
    return pl.pallas_call(
        functools.partial(bank_kernel, rows),
        in_specs=[pl.BlockSpec(memory_space=pl.ANY)],
        out_specs=[spec, spec],
        out_shape=[shape, shape],
        scratch_shapes=[
            pltpu.VMEM(atom_bank.shape, jnp.bfloat16),
            pltpu.VMEM((block * rows, LANES), jnp.float32),
            pltpu.SemaphoreType.DMA((turns, 2)),
        ],
        compiler_params=pltpu.CompilerParams(vmem_limit_bytes=24 * 1024 * 1024),
        name="bank_tiles",
    )(atom_bank)


def conv_kernel(transposed, steps, group, own_ref, beside_ref, even, odd, out_ref, base, spread, total):
    run, parts, width = own_ref.shape
    lanes = width // LANES

    first, second = (own_ref, beside_ref) if transposed else (beside_ref, own_ref)
    base[:, :parts] = first[...].astype(jnp.float32)
    base[:, parts:] = second[...].astype(jnp.float32)

    def fill(shift):
        window = base[:, shift : shift + parts].astype(jnp.bfloat16)
        for lane in range(lanes):
            spread[lane, shift * run : (shift + 1) * run] = window[:, :, lane * LANES : (lane + 1) * LANES]

    def block(step):
        def pair(ref, start):
            return jnp.concatenate([ref[start], ref[start + 1]], axis=1)

        return jnp.concatenate(
            [
                pair(even, 2 * step + 2),
                pair(odd, 2 * step + 1),
                pair(even, 2 * step + 1),
                pair(odd, 2 * step),
            ],
            axis=0,
        )

    def rows(step):
        start = step if transposed else parts * run - step
        return [
            spread[lane, pl.ds(start, run)].reshape(run * parts, LANES) for lane in range(lanes)
        ]

    def product(first, count):
        left = jnp.concatenate([part for i in range(count) for part in rows(first + i)], axis=1)
        if transposed:
            right = jnp.concatenate([block(first + i) for i in range(count)], axis=1)
            dims = (((1,), (1,)), ((), ()))
        else:
            right = jnp.concatenate([block(first + i) for i in range(count)], axis=0)
            dims = (((1,), (0,)), ((), ()))
        return lax.dot_general(left, right, dims, preferred_element_type=jnp.float32)

    order = list(range(parts + 1)) if transposed else list(range(parts, -1, -1))
    if group is None:
        fill(order[0])
        total[0] = product(0, 1)
        total[1] = jnp.zeros_like(total[1])
        for turn in range(parts):
            fill(order[turn + 1])
            total[turn % 2] += product(1 + turn * run, run)
    else:
        for shift in order:
            fill(shift)
        total[...] = jnp.zeros_like(total)

        def loop(turn, carry):
            near = group // 2
            total[0] += product(turn * group, near)
            total[1] += product(turn * group + near, group - near)
            return carry

        turns = steps // group
        lax.fori_loop(0, turns, loop, 0)
        if steps > turns * group:
            total[0] += product(turns * group, steps - turns * group)
    out_ref[...] = (total[0] + total[1]).reshape(out_ref.shape).astype(out_ref.dtype)


def convolve(own, beside, even, odd, transposed, group):
    run, parts, width = own.shape
    tiles, atoms, _ = even.shape
    steps = run * parts + 1
    out_width = PHASES * atoms if transposed else 2 * LANES
    flops = 2 * run * parts * width * out_width * steps
    return pl.pallas_call(
        functools.partial(conv_kernel, transposed, steps, group),
        in_specs=[pl.BlockSpec(memory_space=pltpu.VMEM)] * 4,
        out_specs=pl.BlockSpec(memory_space=pltpu.VMEM),
        out_shape=jax.ShapeDtypeStruct(
            (run, parts, out_width), jnp.float32 if transposed else jnp.bfloat16
        ),
        scratch_shapes=[
            pltpu.VMEM((run, 2 * parts, width), jnp.float32),
            pltpu.VMEM((width // LANES, (parts + 1) * run, parts, LANES), jnp.bfloat16),
            pltpu.VMEM((2, run * parts, out_width), jnp.float32),
        ],
        compiler_params=pltpu.CompilerParams(vmem_limit_bytes=VMEM),
        cost_estimate=pl.CostEstimate(
            flops=flops, bytes_accessed=even.size * 4 + own.size * 8, transcendentals=0
        ),
        name="correlate" if transposed else "synthesize",
    )(own, beside, even, odd)


def shifted(value, axis, steps):
    count = lax.axis_size(axis)
    first, last = max(0, -steps), min(count, count - steps)
    return lax.ppermute(value, axis, [(i, i + steps) for i in range(first, last)])


def summed(value, axis):
    count = lax.axis_size(axis)
    step = 1
    while step < count:
        if step > 1:
            value = value.astype(jnp.bfloat16)
        other = lax.ppermute(value, axis, [(i, i ^ step) for i in range(count)])
        value = value.astype(jnp.float32) + other.astype(jnp.float32)
        step *= 2
    return value


def body(signal, codes_init, atom_bank, step_size, threshold):
    atoms, chans, taps = atom_bank.shape
    held = LANES // 2
    if chans < held:
        atom_bank = jnp.pad(atom_bank, ((0, 0), (0, held - chans), (0, 0)))
        signal = jnp.pad(signal, ((0, held - chans), (0, 0)))
    low, high, heard_low, heard_high = to_blocks(taps, codes_init, signal)
    even, odd = bank_tiles(atom_bank)
    step = jnp.concatenate([step_size] * PHASES)
    bound = jnp.concatenate([step_size * threshold] * PHASES)

    def shrink(current, gradient):
        moved = current - step * gradient
        return moved - jnp.clip(moved, -bound, bound)

    for sweep in range(ITERS):
        group = None if sweep == 0 else 43
        low16, high16 = low.astype(jnp.bfloat16), high.astype(jnp.bfloat16)
        earlier = shifted(high16, "tm", 1)
        recon_high = summed(convolve(high16, low16, even, odd, False, group), "atom")
        recon_low = summed(convolve(low16, earlier, even, odd, False, group), "atom")
        misfit_high = recon_high - heard_high
        misfit_low = recon_low - heard_low
        rounded_high = misfit_high.astype(jnp.bfloat16)
        rounded_low = misfit_low.astype(jnp.bfloat16)
        following = shifted(rounded_low, "tm", -1)
        gradient_low = summed(convolve(rounded_low, rounded_high, even, odd, True, group), "chan")
        gradient_high = summed(convolve(rounded_high, following, even, odd, True, group), "chan")
        low = shrink(low, gradient_low)
        high = shrink(high, gradient_high)
    return from_blocks(low, high), from_blocks(misfit_low, misfit_high)[:chans]


def solution(mesh):
    placed = (P("chan", "tm"), P("atom", "tm"), P("atom", "chan", None), P("atom"), P("atom"))
    return jax.shard_map(
        body,
        mesh=mesh,
        in_specs=placed,
        out_specs=(P("atom", "tm"), P("chan", "tm")),
        check_vma=False,
    )
```

```python
import functools

import jax
import jax.numpy as jnp
from jax import lax
from jax.experimental import pallas as pl
from jax.experimental.pallas import tpu as pltpu
from jax.sharding import PartitionSpec as P

ITERS = 2
PHASES = 4
PARTS = 16
LANES = 128
VMEM = 24 * 1024 * 1024


def blocks_kernel(count, *refs):
    values, outs = refs[:count], refs[count : 3 * count]
    held, flat, sems = refs[3 * count : 4 * count], refs[-2], refs[-1]
    copies = [
        pltpu.make_async_copy(value, place, sems.at[index])
        for index, (value, place) in enumerate(zip(values, held))
    ]
    for copy in copies:
        copy.start()
    for index, value_ref in enumerate(held):
        copies[index].wait()
        halves = outs[2 * index : 2 * index + 2]
        rows, slab = value_ref.shape
        run, parts, _ = halves[0].shape
        length = run * PHASES
        pitch = length + 1
        value = value_ref[...].astype(jnp.float32)
        turned = jnp.concatenate([value, value], axis=0).T
        for part in range(slab // length):
            flat[part * pitch : part * pitch + length] = turned[part * length : (part + 1) * length]
        low = lax.broadcasted_iota(jnp.int32, (parts, LANES), 1) < rows
        for half, out in enumerate(halves):
            for q in range(run):
                first = half * parts * pitch + q * PHASES
                phases = [flat[pl.ds(first + s, parts, stride=pitch), :] for s in range(PHASES)]
                out[q] = jnp.concatenate(
                    [jnp.where(low, phases[s], phases[s + 1]) for s in range(0, PHASES, 2)], axis=1
                )


def to_blocks(taps, *values):
    run = taps // (PHASES * PARTS)
    half = jax.ShapeDtypeStruct((run, PARTS, PHASES * LANES // 2), jnp.float32)
    slab = values[0].shape[1]
    return pl.pallas_call(
        functools.partial(blocks_kernel, len(values)),
        in_specs=[pl.BlockSpec(memory_space=pltpu.HBM)] * len(values),
        out_specs=[pl.BlockSpec(memory_space=pltpu.VMEM)] * (2 * len(values)),
        out_shape=[half] * (2 * len(values)),
        scratch_shapes=[pltpu.VMEM(value.shape, value.dtype) for value in values]
        + [
            pltpu.VMEM((slab + slab // (run * PHASES) + 7, LANES), jnp.float32),
            pltpu.SemaphoreType.DMA((len(values),)),
        ],
        compiler_params=pltpu.CompilerParams(vmem_limit_bytes=VMEM),
        name="to_blocks",
    )(*values)


def series_kernel(low_ref, high_ref, out_ref, flat):
    rows, slab = out_ref.shape
    run, parts, _ = low_ref.shape
    length = run * PHASES
    pitch = length + 1
    for half, value_ref in enumerate((low_ref, high_ref)):
        for q in range(run):
            first = half * parts * pitch + q * PHASES
            for s in range(0, PHASES, 2):
                pair = value_ref[q, :, s // 2 * LANES : (s // 2 + 1) * LANES]
                flat[pl.ds(first + s, parts, stride=pitch), :] = pair
                flat[pl.ds(first + s + 1, parts, stride=pitch), :] = pltpu.roll(pair, LANES // 2, 1)
    turned = jnp.concatenate(
        [flat[part * pitch : part * pitch + length] for part in range(slab // length)], axis=0
    ).T
    out_ref[...] = turned[:rows]


def from_blocks(low, high):
    run, parts, width = low.shape
    slab = 2 * run * parts * PHASES
    return pl.pallas_call(
        series_kernel,
        in_specs=[pl.BlockSpec(memory_space=pltpu.VMEM)] * 2,
        out_specs=pl.BlockSpec(memory_space=pltpu.VMEM),
        out_shape=jax.ShapeDtypeStruct((width // PHASES, slab), jnp.float32),
        scratch_shapes=[pltpu.VMEM((slab + slab // (run * PHASES) + 7, LANES), jnp.float32)],
        compiler_params=pltpu.CompilerParams(vmem_limit_bytes=VMEM),
        name="from_blocks",
    )(low, high)


def bank_kernel(rows, bank_hbm, even_ref, odd_ref, bank, flat, sems):
    atoms, chans, taps = bank.shape
    tiles = even_ref.shape[0]
    half, turns = atoms // 2, sems.shape[0]
    block = half // turns
    margin = 8
    step = min(256, taps)
    eye = (
        lax.broadcasted_iota(jnp.int32, (step, step), 0)
        == lax.broadcasted_iota(jnp.int32, (step, step), 1)
    ).astype(jnp.bfloat16)
    zeros = jnp.zeros((margin, LANES), jnp.float32)
    low = lax.broadcasted_iota(jnp.int32, (block, LANES), 1) < chans

    pieces = sems.shape[1]
    size = block // pieces
    copies = [
        [
            [
                pltpu.make_async_copy(bank_hbm.at[span], bank.at[span], sems.at[group, piece, which])
                for which, span in enumerate(
                    (
                        pl.ds(group * block + piece * size, size),
                        pl.ds(half + group * block + piece * size, size),
                    )
                )
            ]
            for piece in range(pieces)
        ]
        for group in range(turns)
    ]
    for group in copies:
        for piece in group:
            for copy in piece:
                copy.start()

    def tap(index):
        value = flat[pl.ds(index + margin, block, stride=rows), :]
        return value, pltpu.roll(value, chans, 1)

    for group in range(turns):
        def turn(pair, carry):
            first = group * block + 2 * pair
            stacked = jnp.concatenate(
                [bank[first], bank[half + first], bank[first + 1], bank[half + first + 1]], axis=0
            )
            for which in range(2):
                base = (2 * pair + which) * rows
                flat[pl.ds(base, margin), :] = zeros
                flat[pl.ds(base + margin + taps, margin), :] = zeros
            for part in range(taps // step):
                turned = lax.dot_general(
                    eye,
                    stacked[:, part * step : (part + 1) * step],
                    (((1,), (1,)), ((), ())),
                    preferred_element_type=jnp.float32,
                )
                for which in range(2):
                    base = (2 * pair + which) * rows + margin + part * step
                    flat[pl.ds(base, step), :] = turned[:, which * LANES : (which + 1) * LANES]
            return carry

        for piece in range(pieces):
            for copy in copies[group][piece]:
                copy.wait()
            for pair in range(piece * size // 2, (piece + 1) * size // 2):
                turn(pair, 0)

        def store(ref, tile, early, late):
            start = group * block
            ref[tile, start : start + block] = jnp.where(low, early[0], late[1]).astype(jnp.bfloat16)
            start += half
            ref[tile, start : start + block] = jnp.where(low, early[1], late[0]).astype(jnp.bfloat16)

        unroll = next(n for n in (65, 20, 13, 8, 5, 4, 2, 1) if tiles % n == 0)

        def merge(turn_index, carry):
            for inner in range(unroll):
                tile = turn_index * unroll + inner
                middle = tap(2 * tile - 3)
                later = tap(2 * tile - 2)
                store(even_ref, tile, carry, middle)
                store(odd_ref, tile, middle, later)
                carry = later
            return carry

        lax.fori_loop(0, tiles // unroll, merge, tap(-4))


def bank_tiles(atom_bank):
    atoms, chans, taps = atom_bank.shape
    tiles = taps // 2 + 4
    rows = taps + 17
    block = 16
    turns = atoms // 2 // block
    shape = jax.ShapeDtypeStruct((tiles, atoms, LANES), jnp.bfloat16)
    spec = pl.BlockSpec(memory_space=pltpu.VMEM)
    return pl.pallas_call(
        functools.partial(bank_kernel, rows),
        in_specs=[pl.BlockSpec(memory_space=pltpu.HBM)],
        out_specs=[spec, spec],
        out_shape=[shape, shape],
        scratch_shapes=[
            pltpu.VMEM(atom_bank.shape, jnp.bfloat16),
            pltpu.VMEM((block * rows, LANES), jnp.float32),
            pltpu.SemaphoreType.DMA((turns, 4, 2)),
        ],
        compiler_params=pltpu.CompilerParams(vmem_limit_bytes=24 * 1024 * 1024),
        name="bank_tiles",
    )(atom_bank)


def turn_kernel(even_ref, odd_ref, even_out, odd_out):
    tiles = even_ref.shape[0]
    rows = even_out.shape[1]
    eye = (
        lax.broadcasted_iota(jnp.int32, (LANES, LANES), 0)
        == lax.broadcasted_iota(jnp.int32, (LANES, LANES), 1)
    ).astype(jnp.bfloat16)
    unroll = next(n for n in (26, 20, 10, 4, 2) if tiles % n == 0)

    def loop(turn, carry):
        for inner in range(0, unroll, 2):
            tile = turn * unroll + inner
            stacked = jnp.concatenate(
                [odd_ref[tile], even_ref[tile], odd_ref[tile + 1], even_ref[tile + 1]], axis=0
            )
            turned = lax.dot_general(
                eye, stacked, (((1,), (1,)), ((), ())), preferred_element_type=jnp.float32
            ).astype(jnp.bfloat16)
            for which in range(2):
                part = turned[:, which * LANES : (which + 1) * LANES]
                odd_out[tile + which] = part[:rows]
                even_out[tile + which] = part[rows:]
        return carry

    lax.fori_loop(0, tiles // unroll, loop, 0)


def turn_tiles(even, odd):
    tiles = even.shape[0]
    shape = jax.ShapeDtypeStruct((tiles, LANES // 2, LANES), jnp.bfloat16)
    spec = pl.BlockSpec(memory_space=pltpu.VMEM)
    return pl.pallas_call(
        turn_kernel,
        in_specs=[spec, spec],
        out_specs=[spec, spec],
        out_shape=[shape, shape],
        compiler_params=pltpu.CompilerParams(vmem_limit_bytes=VMEM),
        cost_estimate=pl.CostEstimate(
            flops=tiles * LANES**3 * 4, bytes_accessed=4 * even.size * 2, transcendentals=0
        ),
        name="turn_tiles",
    )(even, odd)


def conv_kernel(transposed, steps, own_ref, beside_ref, even, odd, out_ref, base, spread, total):
    run, parts, width = own_ref.shape
    lanes = width // LANES

    first, second = (own_ref, beside_ref) if transposed else (beside_ref, own_ref)
    base[:, :parts] = first[...].astype(jnp.float32)
    base[:, parts:] = second[...].astype(jnp.float32)

    def fill(shift):
        window = base[:, shift : shift + parts].astype(jnp.bfloat16)
        for lane in range(lanes):
            spread[lane, shift * run : (shift + 1) * run] = window[:, :, lane * LANES : (lane + 1) * LANES]

    def block(step):
        if transposed:
            picks = [(even, 1, 0), (odd, 2, 1), (even, 2, 1), (odd, 3, 2)]
        else:
            picks = [(even, 2, 3), (odd, 1, 2), (even, 1, 2), (odd, 0, 1)]
        return jnp.concatenate(
            [
                jnp.concatenate([ref[2 * step + left], ref[2 * step + right]], axis=1)
                for ref, left, right in picks
            ],
            axis=0,
        )

    def rows(step):
        start = step if transposed else parts * run - step
        return [spread[lane, start : start + run].reshape(run * parts, LANES) for lane in range(lanes)]

    def product(first, count):
        left = jnp.concatenate([part for i in range(count) for part in rows(first + i)], axis=1)
        right = jnp.concatenate([block(first + i) for i in range(count)], axis=0)
        return jnp.dot(left, right, preferred_element_type=jnp.float32)

    order = list(range(parts + 1)) if transposed else list(range(parts, -1, -1))
    fill(order[0])
    total[0] = product(0, 1)
    total[1] = jnp.zeros_like(total[1])
    for turn in range(parts):
        fill(order[turn + 1])
        total[turn % 2] += product(1 + turn * run, run)
    out_ref[...] = (total[0] + total[1]).reshape(out_ref.shape).astype(out_ref.dtype)


def convolve(own, beside, tiles, transposed):
    run, parts, width = own.shape
    even, odd = tiles
    steps = run * parts + 1
    out_width = PHASES * LANES // 2
    flops = 2 * run * parts * width * out_width * steps
    return pl.pallas_call(
        functools.partial(conv_kernel, transposed, steps),
        in_specs=[pl.BlockSpec(memory_space=pltpu.VMEM)] * 4,
        out_specs=pl.BlockSpec(memory_space=pltpu.VMEM),
        out_shape=jax.ShapeDtypeStruct(
            (run, parts, out_width), jnp.float32 if transposed else jnp.bfloat16
        ),
        scratch_shapes=[
            pltpu.VMEM((run, 2 * parts, width), jnp.float32),
            pltpu.VMEM((width // LANES, (parts + 1) * run, parts, LANES), jnp.bfloat16),
            pltpu.VMEM((2, run * parts, out_width), jnp.float32),
        ],
        compiler_params=pltpu.CompilerParams(vmem_limit_bytes=VMEM),
        cost_estimate=pl.CostEstimate(
            flops=flops, bytes_accessed=even.size * 4 + own.size * 8, transcendentals=0
        ),
        name="correlate" if transposed else "synthesize",
    )(own, beside, even, odd)


def shifted(value, axis, steps):
    count = lax.axis_size(axis)
    first, last = max(0, -steps), min(count, count - steps)
    return lax.ppermute(value, axis, [(i, i + steps) for i in range(first, last)])


def shifted_by_pairs(value, axis, steps):
    count = lax.axis_size(axis)
    total = None
    for parity in range(2):
        moves = [(i, i + steps) for i in range(count) if 0 <= i + steps < count]
        moves = [move for move in moves if min(move) % 2 == parity]
        if moves:
            part = lax.ppermute(value, axis, moves)
            total = part if total is None else total + part
    return jnp.zeros_like(value) if total is None else total


def summed(value, axis):
    count = lax.axis_size(axis)
    step = 1
    while step < count:
        if step > 1:
            value = value.astype(jnp.bfloat16)
        other = lax.ppermute(value, axis, [(i, i ^ step) for i in range(count)])
        value = value.astype(jnp.float32) + other.astype(jnp.float32)
        step *= 2
    return value


def body(signal, codes_init, atom_bank, step_size, threshold):
    atoms, chans, taps = atom_bank.shape
    held = LANES // 2
    if chans < held:
        atom_bank = jnp.pad(atom_bank, ((0, 0), (0, held - chans), (0, 0)))
        signal = jnp.pad(signal, ((0, held - chans), (0, 0)))
    low, high, heard_low, heard_high = to_blocks(taps, codes_init, signal)
    tiles = bank_tiles(atom_bank)
    step = jnp.concatenate([step_size] * PHASES)
    bound = jnp.concatenate([step_size * threshold] * PHASES)

    def shrink(current, gradient):
        moved = current - step * gradient
        return moved - jnp.clip(moved, -bound, bound)

    turned = None
    for sweep in range(ITERS):
        low16, high16 = low.astype(jnp.bfloat16), high.astype(jnp.bfloat16)
        earlier = shifted(high16, "tm", 1)
        if sweep == 0:
            recon_low = convolve(low16, earlier, tiles, False)
            high16, recon_low = lax.optimization_barrier((high16, recon_low))
            recon_high = convolve(high16, low16, tiles, False)
            turned = turn_tiles(*tiles)
        else:
            recon_high = convolve(high16, low16, tiles, False)
            recon_low = convolve(low16, earlier, tiles, False)
        recon_low, recon_high = summed(recon_low, "atom"), summed(recon_high, "atom")
        misfit_low = recon_low - heard_low
        misfit_high = recon_high - heard_high
        rounded_low = misfit_low.astype(jnp.bfloat16)
        rounded_high = misfit_high.astype(jnp.bfloat16)
        following = shifted_by_pairs(rounded_low, "tm", -1)
        gradient_low = summed(convolve(rounded_low, rounded_high, turned, True), "chan")
        gradient_high = summed(convolve(rounded_high, following, turned, True), "chan")
        low = shrink(low, gradient_low)
        high = shrink(high, gradient_high)
    return from_blocks(low, high), from_blocks(misfit_low, misfit_high)[:chans]


def solution(mesh):
    placed = (P("chan", "tm"), P("atom", "tm"), P("atom", "chan", None), P("atom"), P("atom"))
    return jax.shard_map(
        body,
        mesh=mesh,
        in_specs=placed,
        out_specs=(P("atom", "tm"), P("chan", "tm")),
        check_vma=False,
    )
```

```python
import functools

import jax
import jax.numpy as jnp
from jax import lax
from jax.experimental import pallas as pl
from jax.experimental.pallas import tpu as pltpu
from jax.sharding import PartitionSpec as P

ITERS = 2
PHASES = 4
PARTS = 16
LANES = 128
VMEM = 24 * 1024 * 1024


def blocks_kernel(count, *refs):
    values, outs = refs[:count], refs[count : 3 * count]
    held, flat, sems = refs[3 * count : 4 * count], refs[-2], refs[-1]
    copies = [
        pltpu.make_async_copy(value, place, sems.at[index])
        for index, (value, place) in enumerate(zip(values, held))
    ]
    for copy in copies:
        copy.start()
    for index, value_ref in enumerate(held):
        copies[index].wait()
        halves = outs[2 * index : 2 * index + 2]
        rows, slab = value_ref.shape
        run, parts, _ = halves[0].shape
        length = run * PHASES
        pitch = length + 1
        value = value_ref[...].astype(jnp.float32)
        turned = jnp.concatenate([value, value], axis=0).T
        for part in range(slab // length):
            flat[part * pitch : part * pitch + length] = turned[part * length : (part + 1) * length]
        low = lax.broadcasted_iota(jnp.int32, (parts, LANES), 1) < rows
        for half, out in enumerate(halves):
            for q in range(run):
                first = half * parts * pitch + q * PHASES
                phases = [flat[pl.ds(first + s, parts, stride=pitch), :] for s in range(PHASES)]
                out[q] = jnp.concatenate(
                    [jnp.where(low, phases[s], phases[s + 1]) for s in range(0, PHASES, 2)], axis=1
                )


def to_blocks(taps, *values):
    run = taps // (PHASES * PARTS)
    half = jax.ShapeDtypeStruct((run, PARTS, PHASES * LANES // 2), jnp.float32)
    slab = values[0].shape[1]
    return pl.pallas_call(
        functools.partial(blocks_kernel, len(values)),
        in_specs=[pl.BlockSpec(memory_space=pltpu.HBM)] * len(values),
        out_specs=[pl.BlockSpec(memory_space=pltpu.VMEM)] * (2 * len(values)),
        out_shape=[half] * (2 * len(values)),
        scratch_shapes=[pltpu.VMEM(value.shape, value.dtype) for value in values]
        + [
            pltpu.VMEM((slab + slab // (run * PHASES) + 7, LANES), jnp.float32),
            pltpu.SemaphoreType.DMA((len(values),)),
        ],
        compiler_params=pltpu.CompilerParams(vmem_limit_bytes=VMEM),
        name="to_blocks",
    )(*(pltpu.with_memory_space_constraint(value, pltpu.HBM) for value in values))


def series_kernel(low_ref, high_ref, out_ref, flat):
    rows, slab = out_ref.shape
    run, parts, _ = low_ref.shape
    length = run * PHASES
    pitch = length + 1
    for half, value_ref in enumerate((low_ref, high_ref)):
        for q in range(run):
            first = half * parts * pitch + q * PHASES
            for s in range(0, PHASES, 2):
                pair = value_ref[q, :, s // 2 * LANES : (s // 2 + 1) * LANES]
                flat[pl.ds(first + s, parts, stride=pitch), :] = pair
                flat[pl.ds(first + s + 1, parts, stride=pitch), :] = pltpu.roll(pair, LANES // 2, 1)
    turned = jnp.concatenate(
        [flat[part * pitch : part * pitch + length] for part in range(slab // length)], axis=0
    ).T
    out_ref[...] = turned[:rows]


def from_blocks(low, high):
    run, parts, width = low.shape
    slab = 2 * run * parts * PHASES
    return pl.pallas_call(
        series_kernel,
        in_specs=[pl.BlockSpec(memory_space=pltpu.VMEM)] * 2,
        out_specs=pl.BlockSpec(memory_space=pltpu.VMEM),
        out_shape=jax.ShapeDtypeStruct((width // PHASES, slab), jnp.float32),
        scratch_shapes=[pltpu.VMEM((slab + slab // (run * PHASES) + 7, LANES), jnp.float32)],
        compiler_params=pltpu.CompilerParams(vmem_limit_bytes=VMEM),
        name="from_blocks",
    )(low, high)


def bank_kernel(rows, bank_hbm, even_ref, odd_ref, bank, flat, sems):
    atoms, chans, taps = bank.shape
    tiles = even_ref.shape[0]
    half, turns = atoms // 2, sems.shape[0]
    block = half // turns
    margin = 8
    step = min(256, taps)
    eye = (
        lax.broadcasted_iota(jnp.int32, (step, step), 0)
        == lax.broadcasted_iota(jnp.int32, (step, step), 1)
    ).astype(jnp.bfloat16)
    zeros = jnp.zeros((margin, LANES), jnp.float32)
    low = lax.broadcasted_iota(jnp.int32, (block, LANES), 1) < chans

    pieces = sems.shape[1]
    size = block // pieces
    copies = [
        [
            [
                pltpu.make_async_copy(bank_hbm.at[span], bank.at[span], sems.at[group, piece, which])
                for which, span in enumerate(
                    (
                        pl.ds(group * block + piece * size, size),
                        pl.ds(half + group * block + piece * size, size),
                    )
                )
            ]
            for piece in range(pieces)
        ]
        for group in range(turns)
    ]
    for group in copies:
        for piece in group:
            for copy in piece:
                copy.start()

    def tap(index):
        value = flat[pl.ds(index + margin, block, stride=rows), :]
        return value, pltpu.roll(value, chans, 1)

    for group in range(turns):
        def turn(pair, carry):
            first = group * block + 2 * pair
            stacked = jnp.concatenate(
                [bank[first], bank[half + first], bank[first + 1], bank[half + first + 1]], axis=0
            )
            for which in range(2):
                base = (2 * pair + which) * rows
                flat[pl.ds(base, margin), :] = zeros
                flat[pl.ds(base + margin + taps, margin), :] = zeros
            for part in range(taps // step):
                turned = lax.dot_general(
                    eye,
                    stacked[:, part * step : (part + 1) * step],
                    (((1,), (1,)), ((), ())),
                    preferred_element_type=jnp.float32,
                )
                for which in range(2):
                    base = (2 * pair + which) * rows + margin + part * step
                    flat[pl.ds(base, step), :] = turned[:, which * LANES : (which + 1) * LANES]
            return carry

        for piece in range(pieces):
            for copy in copies[group][piece]:
                copy.wait()
            for pair in range(piece * size // 2, (piece + 1) * size // 2):
                turn(pair, 0)

        def store(ref, tile, early, late):
            start = group * block
            ref[tile, start : start + block] = jnp.where(low, early[0], late[1]).astype(jnp.bfloat16)
            start += half
            ref[tile, start : start + block] = jnp.where(low, early[1], late[0]).astype(jnp.bfloat16)

        unroll = next(n for n in (65, 20, 13, 8, 5, 4, 2, 1) if tiles % n == 0)

        def merge(turn_index, carry):
            for inner in range(unroll):
                tile = turn_index * unroll + inner
                middle = tap(2 * tile - 3)
                later = tap(2 * tile - 2)
                store(even_ref, tile, carry, middle)
                store(odd_ref, tile, middle, later)
                carry = later
            return carry

        lax.fori_loop(0, tiles // unroll, merge, tap(-4))


def bank_tiles(atom_bank):
    atoms, chans, taps = atom_bank.shape
    tiles = taps // 2 + 4
    rows = taps + 17
    block = 16
    turns = atoms // 2 // block
    shape = jax.ShapeDtypeStruct((tiles, atoms, LANES), jnp.bfloat16)
    spec = pl.BlockSpec(memory_space=pltpu.VMEM)
    return pl.pallas_call(
        functools.partial(bank_kernel, rows),
        in_specs=[pl.BlockSpec(memory_space=pltpu.HBM)],
        out_specs=[spec, spec],
        out_shape=[shape, shape],
        scratch_shapes=[
            pltpu.VMEM(atom_bank.shape, jnp.bfloat16),
            pltpu.VMEM((block * rows, LANES), jnp.float32),
            pltpu.SemaphoreType.DMA((turns, 4, 2)),
        ],
        compiler_params=pltpu.CompilerParams(vmem_limit_bytes=24 * 1024 * 1024),
        name="bank_tiles",
    )(pltpu.with_memory_space_constraint(atom_bank, pltpu.HBM))


def turn_kernel(even_ref, odd_ref, even_out, odd_out):
    tiles = even_ref.shape[0]
    rows = even_out.shape[1]
    wide = 2 * LANES
    eye = (
        lax.broadcasted_iota(jnp.int32, (wide, wide), 0)
        == lax.broadcasted_iota(jnp.int32, (wide, wide), 1)
    ).astype(jnp.bfloat16)
    unroll = next(n for n in (52, 20, 4) if tiles % n == 0)

    def loop(turn, carry):
        for inner in range(0, unroll, 4):
            tile = turn * unroll + inner
            stacked = jnp.concatenate(
                [
                    jnp.concatenate([ref[tile + which], ref[tile + 2 + which]], axis=1)
                    for which in range(2)
                    for ref in (odd_ref, even_ref)
                ],
                axis=0,
            )
            turned = lax.dot_general(
                eye, stacked, (((1,), (1,)), ((), ())), preferred_element_type=jnp.float32
            ).astype(jnp.bfloat16)
            for which in range(4):
                part = turned[which // 2 * LANES :, which % 2 * LANES : (which % 2 + 1) * LANES]
                odd_out[tile + which] = part[:rows]
                even_out[tile + which] = part[rows : 2 * rows]
        return carry

    lax.fori_loop(0, tiles // unroll, loop, 0)


def turn_tiles(even, odd):
    tiles = even.shape[0]
    shape = jax.ShapeDtypeStruct((tiles, LANES // 2, LANES), jnp.bfloat16)
    spec = pl.BlockSpec(memory_space=pltpu.VMEM)
    return pl.pallas_call(
        turn_kernel,
        in_specs=[spec, spec],
        out_specs=[spec, spec],
        out_shape=[shape, shape],
        compiler_params=pltpu.CompilerParams(vmem_limit_bytes=VMEM),
        cost_estimate=pl.CostEstimate(
            flops=tiles * LANES**3 * 4, bytes_accessed=4 * even.size * 2, transcendentals=0
        ),
        name="turn_tiles",
    )(even, odd)


def conv_kernel(transposed, steps, own_ref, beside_ref, even, odd, out_ref, base, spread, total):
    run, parts, width = own_ref.shape
    lanes = width // LANES

    first, second = (own_ref, beside_ref) if transposed else (beside_ref, own_ref)
    base[:, :parts] = first[...].astype(jnp.float32)
    base[:, parts:] = second[...].astype(jnp.float32)

    def fill(shift):
        window = base[:, shift : shift + parts].astype(jnp.bfloat16)
        for lane in range(lanes):
            spread[lane, shift * run : (shift + 1) * run] = window[:, :, lane * LANES : (lane + 1) * LANES]

    def block(step):
        if transposed:
            picks = [(even, 1, 0), (odd, 2, 1), (even, 2, 1), (odd, 3, 2)]
        else:
            picks = [(even, 2, 3), (odd, 1, 2), (even, 1, 2), (odd, 0, 1)]
        return jnp.concatenate(
            [
                jnp.concatenate([ref[2 * step + left], ref[2 * step + right]], axis=1)
                for ref, left, right in picks
            ],
            axis=0,
        )

    def rows(step):
        start = step if transposed else parts * run - step
        return [spread[lane, start : start + run].reshape(run * parts, LANES) for lane in range(lanes)]

    def product(first, count):
        left = jnp.concatenate([part for i in range(count) for part in rows(first + i)], axis=1)
        right = jnp.concatenate([block(first + i) for i in range(count)], axis=0)
        return jnp.dot(left, right, preferred_element_type=jnp.float32)

    order = list(range(parts + 1)) if transposed else list(range(parts, -1, -1))
    fill(order[0])
    total[0] = product(0, 1)
    total[1] = jnp.zeros_like(total[1])
    for turn in range(parts):
        fill(order[turn + 1])
        total[turn % 2] += product(1 + turn * run, run)
    out_ref[...] = (total[0] + total[1]).reshape(out_ref.shape).astype(out_ref.dtype)


def convolve(own, beside, tiles, transposed):
    run, parts, width = own.shape
    even, odd = tiles
    steps = run * parts + 1
    out_width = PHASES * LANES // 2
    flops = 2 * run * parts * width * out_width * steps
    return pl.pallas_call(
        functools.partial(conv_kernel, transposed, steps),
        in_specs=[pl.BlockSpec(memory_space=pltpu.VMEM)] * 4,
        out_specs=pl.BlockSpec(memory_space=pltpu.VMEM),
        out_shape=jax.ShapeDtypeStruct(
            (run, parts, out_width), jnp.float32 if transposed else jnp.bfloat16
        ),
        scratch_shapes=[
            pltpu.VMEM((run, 2 * parts, width), jnp.float32),
            pltpu.VMEM((width // LANES, (parts + 1) * run, parts, LANES), jnp.bfloat16),
            pltpu.VMEM((2, run * parts, out_width), jnp.float32),
        ],
        compiler_params=pltpu.CompilerParams(vmem_limit_bytes=VMEM),
        cost_estimate=pl.CostEstimate(
            flops=flops, bytes_accessed=even.size * 4 + own.size * 8, transcendentals=0
        ),
        name="correlate" if transposed else "synthesize",
    )(own, beside, even, odd)


def shifted(value, axis, steps):
    count = lax.axis_size(axis)
    first, last = max(0, -steps), min(count, count - steps)
    return lax.ppermute(value, axis, [(i, i + steps) for i in range(first, last)])


def partner(value, axis, step):
    return lax.ppermute(value, axis, [(i, i ^ step) for i in range(lax.axis_size(axis))])


def after(value, *others):
    return lax.optimization_barrier((value, *others))[0]


def summed(value, axis, gate=None):
    step = 1
    while step < lax.axis_size(axis):
        if step > 1:
            value = value.astype(jnp.bfloat16)
        other = partner(value, axis, step)
        step *= 2
        if gate is not None and step >= lax.axis_size(axis):
            other = after(other, gate)
        value = value.astype(jnp.float32) + other.astype(jnp.float32)
    return value


def summed_both(first, second, axis):
    if lax.axis_size(axis) == 1:
        return first, second
    both = jnp.stack([first + partner(first, axis, 1), second + partner(second, axis, 1)])
    step = 2
    while step < lax.axis_size(axis):
        both = both.astype(jnp.bfloat16)
        other = partner(both, axis, step)
        both = both.astype(jnp.float32) + other.astype(jnp.float32)
        step *= 2
    return both[0], both[1]


def body(signal, codes_init, atom_bank, step_size, threshold):
    atoms, chans, taps = atom_bank.shape
    held = LANES // 2
    if chans < held:
        atom_bank = jnp.pad(atom_bank, ((0, 0), (0, held - chans), (0, 0)))
        signal = jnp.pad(signal, ((0, held - chans), (0, 0)))
    low, high, heard_low, heard_high = to_blocks(taps, codes_init, signal)
    tiles = bank_tiles(atom_bank)
    step = jnp.concatenate([step_size] * PHASES)
    bound = jnp.concatenate([step_size * threshold] * PHASES)

    def shrink(current, gradient):
        moved = current - step * gradient
        return moved - jnp.clip(moved, -bound, bound)

    turned = None
    low16, high16 = low.astype(jnp.bfloat16), high.astype(jnp.bfloat16)
    earlier = shifted(high16, "tm", 1)
    for sweep in range(ITERS):
        recon_low = convolve(low16, earlier, tiles, False)
        recon_high = convolve(after(high16, recon_low), low16, tiles, False)
        misfit_low = summed(recon_low, "atom") - heard_low
        rounded_low = misfit_low.astype(jnp.bfloat16)
        following = shifted(rounded_low, "tm", -1)
        gate = None
        if turned is None:
            turned = turn_tiles(*(after(tile, rounded_low) for tile in tiles))
            gate = turned[0]
        misfit_high = summed(recon_high, "atom", gate) - heard_high
        rounded_high = misfit_high.astype(jnp.bfloat16)
        if sweep < ITERS - 1:
            gradient_high = convolve(rounded_high, following, turned, True)
            gradient_low = convolve(after(rounded_low, gradient_high), rounded_high, turned, True)
            high = shrink(high, summed(gradient_high, "chan"))
            high16 = high.astype(jnp.bfloat16)
            earlier = shifted(high16, "tm", 1)
            low = shrink(low, summed(gradient_low, "chan", earlier))
            low16 = low.astype(jnp.bfloat16)
        else:
            gradient_low = convolve(rounded_low, rounded_high, turned, True)
            gradient_high = convolve(rounded_high, following, turned, True)
            gradient_low, gradient_high = summed_both(gradient_low, gradient_high, "chan")
            low, high = shrink(low, gradient_low), shrink(high, gradient_high)
    return from_blocks(low, high), from_blocks(misfit_low, misfit_high)[:chans]


def solution(mesh):
    placed = (P("chan", "tm"), P("atom", "tm"), P("atom", "chan", None), P("atom"), P("atom"))
    return jax.shard_map(
        body,
        mesh=mesh,
        in_specs=placed,
        out_specs=(P("atom", "tm"), P("chan", "tm")),
        check_vma=False,
    )
```

```python
import functools

import jax
import jax.numpy as jnp
from jax import lax
from jax.experimental import pallas as pl
from jax.experimental.pallas import tpu as pltpu
from jax.sharding import PartitionSpec as P

ITERS = 2
PHASES = 4
PARTS = 16
LANES = 128
VMEM = 24 * 1024 * 1024


def blocks_kernel(count, *refs):
    values, vectors = refs[:count], refs[count : count + 2]
    outs, vector_outs = refs[count + 2 : 3 * count + 2], refs[3 * count + 2 : 3 * count + 4]
    held = refs[3 * count + 4 : 4 * count + 6]
    flat, sems = refs[-2:]
    copies = [
        pltpu.make_async_copy(value, place, sems.at[index])
        for index, (value, place) in enumerate(zip(values + vectors, held))
    ]
    for copy in copies:
        copy.start()
    for index, value_ref in enumerate(held[:count]):
        copies[index].wait()
        halves = outs[2 * index : 2 * index + 2]
        rows, slab = value_ref.shape
        run, parts, _ = halves[0].shape
        length = run * PHASES
        pitch = length + 1
        value = value_ref[...].astype(jnp.float32)
        turned = jnp.concatenate([value, value], axis=0).T
        for part in range(slab // length):
            flat[part * pitch : part * pitch + length] = turned[part * length : (part + 1) * length]
        low = lax.broadcasted_iota(jnp.int32, (parts, LANES), 1) < rows
        for half, out in enumerate(halves):
            for q in range(run):
                first = half * parts * pitch + q * PHASES
                phases = [flat[pl.ds(first + s, parts, stride=pitch), :] for s in range(PHASES)]
                out[q] = jnp.concatenate(
                    [jnp.where(low, phases[s], phases[s + 1]) for s in range(0, PHASES, 2)], axis=1
                )
    for copy in copies[count:]:
        copy.wait()
    step, threshold = held[count][...], held[count + 1][...]
    vector_outs[0][...] = jnp.concatenate([step] * PHASES, axis=1)
    vector_outs[1][...] = jnp.concatenate([step * threshold] * PHASES, axis=1)


def to_blocks(taps, values, vectors):
    run = taps // (PHASES * PARTS)
    width = PHASES * LANES // 2
    half = jax.ShapeDtypeStruct((run, PARTS, width), jnp.float32)
    slab = values[0].shape[1]
    args = [*values, *(vector[None] for vector in vectors)]
    return pl.pallas_call(
        functools.partial(blocks_kernel, len(values)),
        in_specs=[pl.BlockSpec(memory_space=pltpu.HBM)] * len(args),
        out_specs=[pl.BlockSpec(memory_space=pltpu.VMEM)] * (2 * len(values) + 2),
        out_shape=[half] * (2 * len(values)) + [jax.ShapeDtypeStruct((1, width), jnp.float32)] * 2,
        scratch_shapes=[pltpu.VMEM(value.shape, value.dtype) for value in args]
        + [
            pltpu.VMEM((slab + slab // (run * PHASES) + 7, LANES), jnp.float32),
            pltpu.SemaphoreType.DMA((len(args),)),
        ],
        compiler_params=pltpu.CompilerParams(vmem_limit_bytes=VMEM),
        name="to_blocks",
    )(*(pltpu.with_memory_space_constraint(value, pltpu.HBM) for value in args))


def series_kernel(low_ref, high_ref, out_ref, flat):
    rows, slab = out_ref.shape
    run, parts, _ = low_ref.shape
    length = run * PHASES
    pitch = length + 1
    for half, value_ref in enumerate((low_ref, high_ref)):
        for q in range(run):
            first = half * parts * pitch + q * PHASES
            for s in range(0, PHASES, 2):
                pair = value_ref[q, :, s // 2 * LANES : (s // 2 + 1) * LANES]
                flat[pl.ds(first + s, parts, stride=pitch), :] = pair
                flat[pl.ds(first + s + 1, parts, stride=pitch), :] = pltpu.roll(pair, LANES // 2, 1)
    turned = jnp.concatenate(
        [flat[part * pitch : part * pitch + length] for part in range(slab // length)], axis=0
    ).T
    out_ref[...] = turned[:rows]


def from_blocks(low, high):
    run, parts, width = low.shape
    slab = 2 * run * parts * PHASES
    return pl.pallas_call(
        series_kernel,
        in_specs=[pl.BlockSpec(memory_space=pltpu.VMEM)] * 2,
        out_specs=pl.BlockSpec(memory_space=pltpu.VMEM),
        out_shape=jax.ShapeDtypeStruct((width // PHASES, slab), jnp.float32),
        scratch_shapes=[pltpu.VMEM((slab + slab // (run * PHASES) + 7, LANES), jnp.float32)],
        compiler_params=pltpu.CompilerParams(vmem_limit_bytes=VMEM),
        name="from_blocks",
    )(low, high)


def bank_kernel(rows, bank_hbm, even_ref, odd_ref, bank, flat, sems):
    atoms, chans, taps = bank.shape
    tiles = even_ref.shape[0]
    half, turns = atoms // 2, sems.shape[0]
    block = half // turns
    margin = 8
    step = min(256, taps)
    eye = (
        lax.broadcasted_iota(jnp.int32, (step, step), 0)
        == lax.broadcasted_iota(jnp.int32, (step, step), 1)
    ).astype(jnp.bfloat16)
    zeros = jnp.zeros((margin, LANES), jnp.float32)
    low = lax.broadcasted_iota(jnp.int32, (block, LANES), 1) < chans

    pieces = sems.shape[1]
    size = block // pieces
    copies = [
        [
            [
                pltpu.make_async_copy(bank_hbm.at[span], bank.at[span], sems.at[group, piece, which])
                for which, span in enumerate(
                    (
                        pl.ds(group * block + piece * size, size),
                        pl.ds(half + group * block + piece * size, size),
                    )
                )
            ]
            for piece in range(pieces)
        ]
        for group in range(turns)
    ]
    for group in copies:
        for piece in group:
            for copy in piece:
                copy.start()

    def turn(group, pair):
        first = group * block + 2 * pair
        stacked = jnp.concatenate(
            [bank[first], bank[half + first], bank[first + 1], bank[half + first + 1]], axis=0
        )
        place = flat.at[group % 2]
        for which in range(2):
            base = (2 * pair + which) * rows
            place[pl.ds(base, margin), :] = zeros
            place[pl.ds(base + margin + taps, margin), :] = zeros
        for part in range(taps // step):
            turned = lax.dot_general(
                eye,
                stacked[:, part * step : (part + 1) * step],
                (((1,), (1,)), ((), ())),
                preferred_element_type=jnp.float32,
            )
            for which in range(2):
                base = (2 * pair + which) * rows + margin + part * step
                place[pl.ds(base, step), :] = turned[:, which * LANES : (which + 1) * LANES]

    pairs = block // 2
    loops = next(n for n in (4, 2, 1) if tiles % n == 0 and pairs % n == 0)
    unroll, beside = tiles // loops, pairs // loops

    for piece in range(pieces):
        for copy in copies[0][piece]:
            copy.wait()
        for pair in range(piece * size // 2, (piece + 1) * size // 2):
            turn(0, pair)

    for group in range(turns):
        place = flat.at[group % 2]
        start = group * block

        def tap(index):
            value = place[pl.ds(index + margin, block, stride=rows), :]
            return value, pltpu.roll(value, chans, 1)

        def store(ref, tile, early, late):
            ref[tile, start : start + block] = jnp.where(low, early[0], late[1]).astype(jnp.bfloat16)
            ref[tile, half + start : half + start + block] = jnp.where(
                low, early[1], late[0]
            ).astype(jnp.bfloat16)

        if group + 1 < turns:
            for piece in copies[group + 1]:
                for copy in piece:
                    copy.wait()

        def merge(turn_index, carry):
            if group + 1 < turns:
                for inner in range(beside):
                    turn(group + 1, turn_index * beside + inner)
            for inner in range(unroll):
                tile = turn_index * unroll + inner
                middle = tap(2 * tile - 3)
                later = tap(2 * tile - 2)
                store(even_ref, tile, carry, middle)
                store(odd_ref, tile, middle, later)
                carry = later
            return carry

        lax.fori_loop(0, loops, merge, tap(-4))


def bank_tiles(atom_bank):
    atoms, chans, taps = atom_bank.shape
    tiles = taps // 2 + 4
    rows = taps + 17
    block = 16
    turns = atoms // 2 // block
    shape = jax.ShapeDtypeStruct((tiles, atoms, LANES), jnp.bfloat16)
    spec = pl.BlockSpec(memory_space=pltpu.VMEM)
    return pl.pallas_call(
        functools.partial(bank_kernel, rows),
        in_specs=[pl.BlockSpec(memory_space=pltpu.HBM)],
        out_specs=[spec, spec],
        out_shape=[shape, shape],
        scratch_shapes=[
            pltpu.VMEM(atom_bank.shape, jnp.bfloat16),
            pltpu.VMEM((2, block * rows, LANES), jnp.float32),
            pltpu.SemaphoreType.DMA((turns, 4, 2)),
        ],
        compiler_params=pltpu.CompilerParams(vmem_limit_bytes=24 * 1024 * 1024),
        name="bank_tiles",
    )(pltpu.with_memory_space_constraint(atom_bank, pltpu.HBM))


def turn_kernel(even_ref, odd_ref, even_out, odd_out):
    tiles = even_ref.shape[0]
    rows = even_out.shape[1]
    wide = 2 * LANES
    eye = (
        lax.broadcasted_iota(jnp.int32, (wide, wide), 0)
        == lax.broadcasted_iota(jnp.int32, (wide, wide), 1)
    ).astype(jnp.bfloat16)
    unroll = next(n for n in (52, 20, 4) if tiles % n == 0)

    def loop(turn, carry):
        for inner in range(0, unroll, 4):
            tile = turn * unroll + inner
            stacked = jnp.concatenate(
                [
                    jnp.concatenate([ref[tile + which], ref[tile + 2 + which]], axis=1)
                    for which in range(2)
                    for ref in (odd_ref, even_ref)
                ],
                axis=0,
            )
            turned = lax.dot_general(
                eye, stacked, (((1,), (1,)), ((), ())), preferred_element_type=jnp.float32
            ).astype(jnp.bfloat16)
            for which in range(4):
                part = turned[which // 2 * LANES :, which % 2 * LANES : (which % 2 + 1) * LANES]
                odd_out[tile + which] = part[:rows]
                even_out[tile + which] = part[rows : 2 * rows]
        return carry

    lax.fori_loop(0, tiles // unroll, loop, 0)


def turn_tiles(even, odd):
    tiles = even.shape[0]
    shape = jax.ShapeDtypeStruct((tiles, LANES // 2, LANES), jnp.bfloat16)
    spec = pl.BlockSpec(memory_space=pltpu.VMEM)
    return pl.pallas_call(
        turn_kernel,
        in_specs=[spec, spec],
        out_specs=[spec, spec],
        out_shape=[shape, shape],
        compiler_params=pltpu.CompilerParams(vmem_limit_bytes=VMEM),
        cost_estimate=pl.CostEstimate(
            flops=tiles * LANES**3 * 4, bytes_accessed=4 * even.size * 2, transcendentals=0
        ),
        name="turn_tiles",
    )(even, odd)


def conv_kernel(transposed, steps, own_ref, beside_ref, even, odd, out_ref, base, spread, total):
    run, parts, width = own_ref.shape
    lanes = width // LANES

    first, second = (own_ref, beside_ref) if transposed else (beside_ref, own_ref)
    base[:, :parts] = first[...].astype(jnp.float32)
    base[:, parts:] = second[...].astype(jnp.float32)

    def fill(shift):
        window = base[:, shift : shift + parts].astype(jnp.bfloat16)
        for lane in range(lanes):
            spread[lane, shift * run : (shift + 1) * run] = window[:, :, lane * LANES : (lane + 1) * LANES]

    def block(step):
        if transposed:
            picks = [(even, 1, 0), (odd, 2, 1), (even, 2, 1), (odd, 3, 2)]
        else:
            picks = [(even, 2, 3), (odd, 1, 2), (even, 1, 2), (odd, 0, 1)]
        return jnp.concatenate(
            [
                jnp.concatenate([ref[2 * step + left], ref[2 * step + right]], axis=1)
                for ref, left, right in picks
            ],
            axis=0,
        )

    def rows(step):
        start = step if transposed else parts * run - step
        return [spread[lane, start : start + run].reshape(run * parts, LANES) for lane in range(lanes)]

    def product(first, count):
        left = jnp.concatenate([part for i in range(count) for part in rows(first + i)], axis=1)
        right = jnp.concatenate([block(first + i) for i in range(count)], axis=0)
        return jnp.dot(left, right, preferred_element_type=jnp.float32)

    order = list(range(parts + 1)) if transposed else list(range(parts, -1, -1))
    fill(order[0])
    total[0] = product(0, 1)
    total[1] = jnp.zeros_like(total[1])
    for turn in range(parts):
        fill(order[turn + 1])
        total[turn % 2] += product(1 + turn * run, run)
    out_ref[...] = (total[0] + total[1]).reshape(out_ref.shape).astype(out_ref.dtype)


def convolve(own, beside, tiles, transposed):
    run, parts, width = own.shape
    even, odd = tiles
    steps = run * parts + 1
    out_width = PHASES * LANES // 2
    flops = 2 * run * parts * width * out_width * steps
    return pl.pallas_call(
        functools.partial(conv_kernel, transposed, steps),
        in_specs=[pl.BlockSpec(memory_space=pltpu.VMEM)] * 4,
        out_specs=pl.BlockSpec(memory_space=pltpu.VMEM),
        out_shape=jax.ShapeDtypeStruct(
            (run, parts, out_width), jnp.float32 if transposed else jnp.bfloat16
        ),
        scratch_shapes=[
            pltpu.VMEM((run, 2 * parts, width), jnp.float32),
            pltpu.VMEM((width // LANES, (parts + 1) * run, parts, LANES), jnp.bfloat16),
            pltpu.VMEM((2, run * parts, out_width), jnp.float32),
        ],
        compiler_params=pltpu.CompilerParams(vmem_limit_bytes=VMEM),
        cost_estimate=pl.CostEstimate(
            flops=flops, bytes_accessed=even.size * 4 + own.size * 8, transcendentals=0
        ),
        name="correlate" if transposed else "synthesize",
    )(own, beside, even, odd)


def shifted(value, axis, steps, closed):
    count = lax.axis_size(axis)
    if count == 1:
        return jnp.zeros_like(value)
    swaps = [(i, i ^ 1) for i in range(count)]
    inner = [(i, i + 1) for i in range(1, count - 1, 2)]
    inner += [(j, i) for i, j in inner]
    if closed and count > 2:
        inner += [(0, count - 1), (count - 1, 0)]
    first = lax.ppermute(value, axis, swaps)
    second = lax.ppermute(value, axis, inner) if inner else jnp.zeros_like(value)
    place = lax.axis_index(axis)
    source = place - steps
    second = jnp.where((source >= 0) & (source < count), second, 0)
    return jnp.where(source == (place ^ 1), first, second)


def partner(value, axis, step):
    return lax.ppermute(value, axis, [(i, i ^ step) for i in range(lax.axis_size(axis))])


def after(value, *others):
    return lax.optimization_barrier((value, *others))[0]


def summed(value, axis, gate=None):
    step = 1
    while step < lax.axis_size(axis):
        if step > 1:
            value = value.astype(jnp.bfloat16)
        other = partner(value, axis, step)
        step *= 2
        if gate is not None and step >= lax.axis_size(axis):
            other = after(other, gate)
        value = value.astype(jnp.float32) + other.astype(jnp.float32)
    return value


def body(signal, codes_init, atom_bank, step_size, threshold):
    atoms, chans, taps = atom_bank.shape
    held = LANES // 2
    if chans < held:
        atom_bank = jnp.pad(atom_bank, ((0, 0), (0, held - chans), (0, 0)))
        signal = jnp.pad(signal, ((0, held - chans), (0, 0)))
    low, high, heard_low, heard_high, step, bound = to_blocks(
        taps, (codes_init, signal), (step_size, threshold)
    )
    tiles = bank_tiles(atom_bank)

    def shrink(current, gradient):
        moved = current - step * gradient
        return moved - jnp.clip(moved, -bound, bound)

    turned = None
    low16, high16 = low.astype(jnp.bfloat16), high.astype(jnp.bfloat16)
    earlier = shifted(high16, "tm", 1, False)
    for sweep in range(ITERS):
        recon_low = convolve(low16, earlier, tiles, False)
        recon_high = convolve(after(high16, recon_low), low16, tiles, False)
        misfit_low = summed(recon_low, "atom") - heard_low
        rounded_low = misfit_low.astype(jnp.bfloat16)
        following = shifted(rounded_low, "tm", -1, True)
        gate = None
        if turned is None:
            turned = turn_tiles(*(after(tile, rounded_low) for tile in tiles))
            gate = turned[0]
        misfit_high = summed(recon_high, "atom", gate) - heard_high
        rounded_high = misfit_high.astype(jnp.bfloat16)
        if sweep < ITERS - 1:
            gradient_high = convolve(rounded_high, following, turned, True)
            gradient_low = convolve(after(rounded_low, gradient_high), rounded_high, turned, True)
            high = shrink(high, summed(gradient_high, "chan"))
            high16 = high.astype(jnp.bfloat16)
            earlier = shifted(high16, "tm", 1, False)
            low = shrink(low, summed(gradient_low, "chan", earlier))
            low16 = low.astype(jnp.bfloat16)
        else:
            gradient_low = convolve(rounded_low, rounded_high, turned, True)
            gradient_high = convolve(rounded_high, following, turned, True)
            low = shrink(low, summed(gradient_low, "chan"))
            high = shrink(high, summed(gradient_high, "chan"))
    return from_blocks(low, high), from_blocks(misfit_low, misfit_high)[:chans]


def solution(mesh):
    placed = (P("chan", "tm"), P("atom", "tm"), P("atom", "chan", None), P("atom"), P("atom"))
    return jax.shard_map(
        body,
        mesh=mesh,
        in_specs=placed,
        out_specs=(P("atom", "tm"), P("chan", "tm")),
        check_vma=False,
    )
```

```python
import functools

import jax
import jax.numpy as jnp
from jax import lax
from jax.experimental import pallas as pl
from jax.experimental.pallas import tpu as pltpu
from jax.sharding import PartitionSpec as P

ITERS = 2
PHASES = 4
PARTS = 16
LANES = 128
VMEM = 24 * 1024 * 1024


def blocks_kernel(count, *refs):
    values, vectors = refs[:count], refs[count : count + 2]
    outs, vector_outs = refs[count + 2 : 3 * count + 2], refs[3 * count + 2 : 3 * count + 4]
    held = refs[3 * count + 4 : 4 * count + 6]
    flat, sems = refs[-2:]
    copies = [
        pltpu.make_async_copy(value, place, sems.at[index])
        for index, (value, place) in enumerate(zip(values + vectors, held))
    ]
    for copy in copies:
        copy.start()
    for index, value_ref in enumerate(held[:count]):
        copies[index].wait()
        halves = outs[2 * index : 2 * index + 2]
        rows, slab = value_ref.shape
        run, parts, _ = halves[0].shape
        length = run * PHASES
        pitch = length + 1
        value = value_ref[...].astype(jnp.float32)
        turned = jnp.concatenate([value, value], axis=0).T
        for part in range(slab // length):
            flat[part * pitch : part * pitch + length] = turned[part * length : (part + 1) * length]
        low = lax.broadcasted_iota(jnp.int32, (parts, LANES), 1) < rows
        for half, out in enumerate(halves):
            for q in range(run):
                first = half * parts * pitch + q * PHASES
                phases = [flat[pl.ds(first + s, parts, stride=pitch), :] for s in range(PHASES)]
                out[q] = jnp.concatenate(
                    [jnp.where(low, phases[s], phases[s + 1]) for s in range(0, PHASES, 2)], axis=1
                )
    for copy in copies[count:]:
        copy.wait()
    step, threshold = held[count][...], held[count + 1][...]
    vector_outs[0][...] = jnp.concatenate([step] * PHASES, axis=1)
    vector_outs[1][...] = jnp.concatenate([step * threshold] * PHASES, axis=1)


def to_blocks(taps, values, vectors):
    run = taps // (PHASES * PARTS)
    width = PHASES * LANES // 2
    half = jax.ShapeDtypeStruct((run, PARTS, width), jnp.float32)
    slab = values[0].shape[1]
    args = [*values, *(vector[None] for vector in vectors)]
    return pl.pallas_call(
        functools.partial(blocks_kernel, len(values)),
        in_specs=[pl.BlockSpec(memory_space=pltpu.HBM)] * len(args),
        out_specs=[pl.BlockSpec(memory_space=pltpu.VMEM)] * (2 * len(values) + 2),
        out_shape=[half] * (2 * len(values)) + [jax.ShapeDtypeStruct((1, width), jnp.float32)] * 2,
        scratch_shapes=[pltpu.VMEM(value.shape, value.dtype) for value in args]
        + [
            pltpu.VMEM((slab + slab // (run * PHASES) + 7, LANES), jnp.float32),
            pltpu.SemaphoreType.DMA((len(args),)),
        ],
        compiler_params=pltpu.CompilerParams(vmem_limit_bytes=VMEM),
        name="to_blocks",
    )(*(pltpu.with_memory_space_constraint(value, pltpu.HBM) for value in args))


def series_kernel(low_ref, high_ref, out_ref, flat):
    rows, slab = out_ref.shape
    run, parts, _ = low_ref.shape
    length = run * PHASES
    pitch = length + 1
    for half, value_ref in enumerate((low_ref, high_ref)):
        for q in range(run):
            first = half * parts * pitch + q * PHASES
            for s in range(0, PHASES, 2):
                pair = value_ref[q, :, s // 2 * LANES : (s // 2 + 1) * LANES]
                flat[pl.ds(first + s, parts, stride=pitch), :] = pair
                flat[pl.ds(first + s + 1, parts, stride=pitch), :] = pltpu.roll(pair, LANES // 2, 1)
    turned = jnp.concatenate(
        [flat[part * pitch : part * pitch + length] for part in range(slab // length)], axis=0
    ).T
    out_ref[...] = turned[:rows]


def from_blocks(low, high):
    run, parts, width = low.shape
    slab = 2 * run * parts * PHASES
    return pl.pallas_call(
        series_kernel,
        in_specs=[pl.BlockSpec(memory_space=pltpu.VMEM)] * 2,
        out_specs=pl.BlockSpec(memory_space=pltpu.VMEM),
        out_shape=jax.ShapeDtypeStruct((width // PHASES, slab), jnp.float32),
        scratch_shapes=[pltpu.VMEM((slab + slab // (run * PHASES) + 7, LANES), jnp.float32)],
        compiler_params=pltpu.CompilerParams(vmem_limit_bytes=VMEM),
        name="from_blocks",
    )(low, high)


def bank_kernel(rows, bank_hbm, even_ref, odd_ref, bank, flat, sems):
    atoms, chans, taps = bank.shape
    tiles = even_ref.shape[0]
    half, turns = atoms // 2, sems.shape[0]
    block = half // turns
    margin = 8
    step = min(256, taps)
    eye = (
        lax.broadcasted_iota(jnp.int32, (step, step), 0)
        == lax.broadcasted_iota(jnp.int32, (step, step), 1)
    ).astype(jnp.bfloat16)
    zeros = jnp.zeros((margin, LANES), jnp.float32)
    low = lax.broadcasted_iota(jnp.int32, (block, LANES), 1) < chans

    pieces = sems.shape[1]
    size = block // pieces
    copies = [
        [
            [
                pltpu.make_async_copy(bank_hbm.at[span], bank.at[span], sems.at[group, piece, which])
                for which, span in enumerate(
                    (
                        pl.ds(group * block + piece * size, size),
                        pl.ds(half + group * block + piece * size, size),
                    )
                )
            ]
            for piece in range(pieces)
        ]
        for group in range(turns)
    ]
    for group in copies:
        for piece in group:
            for copy in piece:
                copy.start()

    def turn(group, pair):
        first = group * block + 2 * pair
        stacked = jnp.concatenate(
            [bank[first], bank[half + first], bank[first + 1], bank[half + first + 1]], axis=0
        )
        place = flat.at[group % 2]
        for which in range(2):
            base = (2 * pair + which) * rows
            place[pl.ds(base, margin), :] = zeros
            place[pl.ds(base + margin + taps, margin), :] = zeros
        for part in range(taps // step):
            turned = lax.dot_general(
                eye,
                stacked[:, part * step : (part + 1) * step],
                (((1,), (1,)), ((), ())),
                preferred_element_type=jnp.float32,
            )
            for which in range(2):
                base = (2 * pair + which) * rows + margin + part * step
                place[pl.ds(base, step), :] = turned[:, which * LANES : (which + 1) * LANES]

    pairs = block // 2
    for piece in range(pieces):
        for copy in copies[0][piece]:
            copy.wait()
        for pair in range(piece * size // 2, (piece + 1) * size // 2):
            turn(0, pair)

    for group in range(turns):
        place = flat.at[group % 2]
        start = group * block

        def tap(index):
            value = place[pl.ds(index + margin, block, stride=rows), :]
            return value, pltpu.roll(value, chans, 1)

        def store(ref, tile, early, late):
            ref[tile, start : start + block] = jnp.where(low, early[0], late[1]).astype(jnp.bfloat16)
            ref[tile, half + start : half + start + block] = jnp.where(
                low, early[1], late[0]
            ).astype(jnp.bfloat16)

        if group + 1 < turns:
            for piece in copies[group + 1]:
                for copy in piece:
                    copy.wait()

        early = tap(-4)
        for tile in range(tiles):
            if group + 1 < turns and tile % (tiles // pairs) == 0 and tile // (tiles // pairs) < pairs:
                turn(group + 1, tile // (tiles // pairs))
            middle = tap(2 * tile - 3)
            late = tap(2 * tile - 2)
            store(even_ref, tile, early, middle)
            store(odd_ref, tile, middle, late)
            early = late


def bank_tiles(atom_bank):
    atoms, chans, taps = atom_bank.shape
    tiles = taps // 2 + 4
    rows = taps + 17
    block = 16
    turns = atoms // 2 // block
    shape = jax.ShapeDtypeStruct((tiles, atoms, LANES), jnp.bfloat16)
    spec = pl.BlockSpec(memory_space=pltpu.VMEM)
    return pl.pallas_call(
        functools.partial(bank_kernel, rows),
        in_specs=[pl.BlockSpec(memory_space=pltpu.HBM)],
        out_specs=[spec, spec],
        out_shape=[shape, shape],
        scratch_shapes=[
            pltpu.VMEM(atom_bank.shape, jnp.bfloat16),
            pltpu.VMEM((2, block * rows, LANES), jnp.float32),
            pltpu.SemaphoreType.DMA((turns, 4, 2)),
        ],
        compiler_params=pltpu.CompilerParams(vmem_limit_bytes=24 * 1024 * 1024),
        name="bank_tiles",
    )(pltpu.with_memory_space_constraint(atom_bank, pltpu.HBM))


def turn_kernel(even_ref, odd_ref, even_out, odd_out):
    tiles = even_ref.shape[0]
    rows = even_out.shape[1]
    wide = 2 * LANES
    eye = (
        lax.broadcasted_iota(jnp.int32, (wide, wide), 0)
        == lax.broadcasted_iota(jnp.int32, (wide, wide), 1)
    ).astype(jnp.bfloat16)
    unroll = next(n for n in (260, 52, 20, 4) if tiles % n == 0)

    def loop(turn, carry):
        for inner in range(0, unroll, 4):
            tile = turn * unroll + inner
            stacked = jnp.concatenate(
                [
                    jnp.concatenate([ref[tile + which], ref[tile + 2 + which]], axis=1)
                    for which in range(2)
                    for ref in (odd_ref, even_ref)
                ],
                axis=0,
            )
            turned = lax.dot_general(
                eye, stacked, (((1,), (1,)), ((), ())), preferred_element_type=jnp.float32
            ).astype(jnp.bfloat16)
            for which in range(4):
                part = turned[which // 2 * LANES :, which % 2 * LANES : (which % 2 + 1) * LANES]
                odd_out[tile + which] = part[:rows]
                even_out[tile + which] = part[rows : 2 * rows]
        return carry

    lax.fori_loop(0, tiles // unroll, loop, 0)


def turn_tiles(even, odd):
    tiles = even.shape[0]
    shape = jax.ShapeDtypeStruct((tiles, LANES // 2, LANES), jnp.bfloat16)
    spec = pl.BlockSpec(memory_space=pltpu.VMEM)
    return pl.pallas_call(
        turn_kernel,
        in_specs=[spec, spec],
        out_specs=[spec, spec],
        out_shape=[shape, shape],
        compiler_params=pltpu.CompilerParams(vmem_limit_bytes=VMEM),
        cost_estimate=pl.CostEstimate(
            flops=tiles * LANES**3 * 4, bytes_accessed=4 * even.size * 2, transcendentals=0
        ),
        name="turn_tiles",
    )(even, odd)


def conv_kernel(transposed, edge, own_ref, beside_ref, even, odd, out_ref, base, spread, total):
    run, parts, width = own_ref.shape
    lanes = width // LANES

    beside = beside_ref[...].astype(jnp.float32)
    if edge is not None:
        axis, last = edge
        beside = jnp.where(lax.axis_index(axis) == last, 0.0, beside)
    own_start = 0 if transposed else parts
    base[:, own_start : own_start + parts] = own_ref[...].astype(jnp.float32)
    base[:, parts - own_start : 2 * parts - own_start] = beside

    def fill(shift):
        window = base[:, shift : shift + parts].astype(jnp.bfloat16)
        for lane in range(lanes):
            spread[lane, shift * run : (shift + 1) * run] = window[:, :, lane * LANES : (lane + 1) * LANES]

    def block(step):
        if transposed:
            picks = [(even, 1, 0), (odd, 2, 1), (even, 2, 1), (odd, 3, 2)]
        else:
            picks = [(even, 2, 3), (odd, 1, 2), (even, 1, 2), (odd, 0, 1)]
        return jnp.concatenate(
            [
                jnp.concatenate([ref[2 * step + left], ref[2 * step + right]], axis=1)
                for ref, left, right in picks
            ],
            axis=0,
        )

    def rows(step):
        start = step if transposed else parts * run - step
        return [spread[lane, start : start + run].reshape(run * parts, LANES) for lane in range(lanes)]

    def product(first, count):
        left = jnp.concatenate([part for i in range(count) for part in rows(first + i)], axis=1)
        right = jnp.concatenate([block(first + i) for i in range(count)], axis=0)
        return jnp.dot(left, right, preferred_element_type=jnp.float32)

    order = list(range(parts + 1)) if transposed else list(range(parts, -1, -1))
    fill(order[0])
    total[0] = product(0, 1)
    total[1] = jnp.zeros_like(total[1])
    for turn in range(0, parts, 2):
        fill(order[turn + 1])
        fill(order[turn + 2])
        total[turn // 2 % 2] += product(1 + turn * run, 2 * run)
    out_ref[...] = (total[0] + total[1]).reshape(out_ref.shape).astype(out_ref.dtype)


def convolve(own, beside, tiles, transposed, edge=None):
    run, parts, width = own.shape
    even, odd = tiles
    steps = run * parts + 1
    out_width = PHASES * LANES // 2
    flops = 2 * run * parts * width * out_width * steps
    return pl.pallas_call(
        functools.partial(conv_kernel, transposed, edge),
        in_specs=[pl.BlockSpec(memory_space=pltpu.VMEM)] * 4,
        out_specs=pl.BlockSpec(memory_space=pltpu.VMEM),
        out_shape=jax.ShapeDtypeStruct((run, parts, out_width), jnp.bfloat16),
        scratch_shapes=[
            pltpu.VMEM((run, 2 * parts, width), jnp.float32),
            pltpu.VMEM((width // LANES, (parts + 1) * run, parts, LANES), jnp.bfloat16),
            pltpu.VMEM((2, run * parts, out_width), jnp.float32),
        ],
        compiler_params=pltpu.CompilerParams(vmem_limit_bytes=VMEM),
        cost_estimate=pl.CostEstimate(
            flops=flops, bytes_accessed=even.size * 4 + own.size * 8, transcendentals=0
        ),
        name="correlate" if transposed else "synthesize",
    )(own, beside, even, odd)


def shifted(value, axis, steps):
    count = lax.axis_size(axis)
    if count == 1:
        return jnp.zeros_like(value)
    return lax.ppermute(value, axis, [(i, (i + steps) % count) for i in range(count)])


def partner(value, axis, step):
    return lax.ppermute(value, axis, [(i, i ^ step) for i in range(lax.axis_size(axis))])


def after(value, *others):
    return lax.optimization_barrier((value, *others))[0]


def summed(value, axis, gate=None):
    step = lax.axis_size(axis) // 2
    while step:
        if step > 1:
            value = value.astype(jnp.bfloat16)
        other = partner(value, axis, step)
        step //= 2
        if gate is not None and not step:
            other = after(other, gate)
        value = value.astype(jnp.float32) + other.astype(jnp.float32)
    return value


def body(signal, codes_init, atom_bank, step_size, threshold):
    atoms, chans, taps = atom_bank.shape
    held = LANES // 2
    if chans < held:
        atom_bank = jnp.pad(atom_bank, ((0, 0), (0, held - chans), (0, 0)))
        signal = jnp.pad(signal, ((0, held - chans), (0, 0)))
    low, high, heard_low, heard_high, step, bound = to_blocks(
        taps, (codes_init, signal), (step_size, threshold)
    )
    tiles = bank_tiles(atom_bank)

    def shrink(current, gradient):
        moved = current - step * gradient
        return moved - jnp.clip(moved, -bound, bound)

    last = lax.axis_size("tm") - 1
    turned = None
    low16, high16 = low.astype(jnp.bfloat16), high.astype(jnp.bfloat16)
    earlier = shifted(high16, "tm", 1)
    for sweep in range(ITERS):
        recon_low = convolve(low16, earlier, tiles, False, ("tm", 0))
        recon_high = convolve(after(high16, recon_low), low16, tiles, False)
        misfit_low = summed(recon_low, "atom") - heard_low
        rounded_low = misfit_low.astype(jnp.bfloat16)
        following = shifted(rounded_low, "tm", -1)
        gate = None
        if turned is None:
            turned = turn_tiles(*(after(tile, rounded_low) for tile in tiles))
            gate = turned[0]
        misfit_high = summed(recon_high, "atom", gate) - heard_high
        rounded_high = misfit_high.astype(jnp.bfloat16)
        if sweep < ITERS - 1:
            gradient_high = convolve(rounded_high, following, turned, True, ("tm", last))
            gradient_low = convolve(after(rounded_low, gradient_high), rounded_high, turned, True)
            high = shrink(high, summed(gradient_high, "chan"))
            high16 = high.astype(jnp.bfloat16)
            earlier = shifted(high16, "tm", 1)
            low = shrink(low, summed(gradient_low, "chan", earlier))
            low16 = low.astype(jnp.bfloat16)
        else:
            gradient_low = convolve(rounded_low, rounded_high, turned, True)
            gradient_high = convolve(rounded_high, following, turned, True, ("tm", last))
            low = shrink(low, summed(gradient_low, "chan"))
            high = shrink(high, summed(gradient_high, "chan"))
    return from_blocks(low, high), from_blocks(misfit_low, misfit_high)[:chans]


def solution(mesh):
    placed = (P("chan", "tm"), P("atom", "tm"), P("atom", "chan", None), P("atom"), P("atom"))
    return jax.shard_map(
        body,
        mesh=mesh,
        in_specs=placed,
        out_specs=(P("atom", "tm"), P("chan", "tm")),
        check_vma=False,
    )
```

```python
import functools

import jax
import jax.numpy as jnp
from jax import lax
from jax.experimental import pallas as pl
from jax.experimental.pallas import tpu as pltpu
from jax.sharding import PartitionSpec as P

ITERS = 2
PHASES = 4
PARTS = 16
LANES = 128
VMEM = 24 * 1024 * 1024


def blocks_kernel(count, *refs):
    values, vectors = refs[:count], refs[count : count + 2]
    outs, vector_outs = refs[count + 2 : 3 * count + 2], refs[3 * count + 2 : 3 * count + 4]
    held = refs[3 * count + 4 : 4 * count + 6]
    flat, sems = refs[-2:]
    copies = [
        pltpu.make_async_copy(value, place, sems.at[index])
        for index, (value, place) in enumerate(zip(values + vectors, held))
    ]
    for copy in copies:
        copy.start()
    for index, value_ref in enumerate(held[:count]):
        copies[index].wait()
        halves = outs[2 * index : 2 * index + 2]
        rows, slab = value_ref.shape
        run, parts, _ = halves[0].shape
        length = run * PHASES
        pitch = length + 1
        value = value_ref[...].astype(jnp.float32)
        turned = jnp.concatenate([value, value], axis=0).T
        for part in range(slab // length):
            flat[part * pitch : part * pitch + length] = turned[part * length : (part + 1) * length]
        low = lax.broadcasted_iota(jnp.int32, (parts, LANES), 1) < rows
        for half, out in enumerate(halves):
            for q in range(run):
                first = half * parts * pitch + q * PHASES
                phases = [flat[pl.ds(first + s, parts, stride=pitch), :] for s in range(PHASES)]
                out[q] = jnp.concatenate(
                    [jnp.where(low, phases[s], phases[s + 1]) for s in range(0, PHASES, 2)], axis=1
                )
    for copy in copies[count:]:
        copy.wait()
    step, threshold = held[count][...], held[count + 1][...]
    vector_outs[0][...] = jnp.concatenate([step] * PHASES, axis=1)
    vector_outs[1][...] = jnp.concatenate([step * threshold] * PHASES, axis=1)


def to_blocks(taps, values, vectors):
    run = taps // (PHASES * PARTS)
    width = PHASES * LANES // 2
    half = jax.ShapeDtypeStruct((run, PARTS, width), jnp.float32)
    slab = values[0].shape[1]
    args = [*values, *(vector[None] for vector in vectors)]
    return pl.pallas_call(
        functools.partial(blocks_kernel, len(values)),
        in_specs=[pl.BlockSpec(memory_space=pltpu.HBM)] * len(args),
        out_specs=[pl.BlockSpec(memory_space=pltpu.VMEM)] * (2 * len(values) + 2),
        out_shape=[half] * (2 * len(values)) + [jax.ShapeDtypeStruct((1, width), jnp.float32)] * 2,
        scratch_shapes=[pltpu.VMEM(value.shape, value.dtype) for value in args]
        + [
            pltpu.VMEM((slab + slab // (run * PHASES) + 7, LANES), jnp.float32),
            pltpu.SemaphoreType.DMA((len(args),)),
        ],
        compiler_params=pltpu.CompilerParams(vmem_limit_bytes=VMEM),
        name="to_blocks",
    )(*(pltpu.with_memory_space_constraint(value, pltpu.HBM) for value in args))


def series_kernel(low_ref, high_ref, out_ref, flat):
    rows, slab = out_ref.shape
    run, parts, _ = low_ref.shape
    length = run * PHASES
    pitch = length + 1
    for half, value_ref in enumerate((low_ref, high_ref)):
        for q in range(run):
            first = half * parts * pitch + q * PHASES
            for s in range(0, PHASES, 2):
                pair = value_ref[q, :, s // 2 * LANES : (s // 2 + 1) * LANES]
                flat[pl.ds(first + s, parts, stride=pitch), :] = pair
                flat[pl.ds(first + s + 1, parts, stride=pitch), :] = pltpu.roll(pair, LANES // 2, 1)
    turned = jnp.concatenate(
        [flat[part * pitch : part * pitch + length] for part in range(slab // length)], axis=0
    ).T
    out_ref[...] = turned[:rows]


def from_blocks(low, high):
    run, parts, width = low.shape
    slab = 2 * run * parts * PHASES
    return pl.pallas_call(
        series_kernel,
        in_specs=[pl.BlockSpec(memory_space=pltpu.VMEM)] * 2,
        out_specs=pl.BlockSpec(memory_space=pltpu.VMEM),
        out_shape=jax.ShapeDtypeStruct((width // PHASES, slab), jnp.float32),
        scratch_shapes=[pltpu.VMEM((slab + slab // (run * PHASES) + 7, LANES), jnp.float32)],
        compiler_params=pltpu.CompilerParams(vmem_limit_bytes=VMEM),
        name="from_blocks",
    )(low, high)


def bank_kernel(rows, bank_hbm, even_ref, odd_ref, bank, flat, sems):
    atoms, chans, taps = bank.shape
    tiles = even_ref.shape[0]
    half, turns = atoms // 2, sems.shape[0]
    block = half // turns
    margin = 8
    step = min(256, taps)
    eye = (
        lax.broadcasted_iota(jnp.int32, (step, step), 0)
        == lax.broadcasted_iota(jnp.int32, (step, step), 1)
    ).astype(jnp.bfloat16)
    zeros = jnp.zeros((margin, LANES), jnp.float32)
    low = lax.broadcasted_iota(jnp.int32, (block, LANES), 1) < chans

    pieces = sems.shape[1]
    size = block // pieces
    copies = [
        [
            [
                pltpu.make_async_copy(bank_hbm.at[span], bank.at[span], sems.at[group, piece, which])
                for which, span in enumerate(
                    (
                        pl.ds(group * block + piece * size, size),
                        pl.ds(half + group * block + piece * size, size),
                    )
                )
            ]
            for piece in range(pieces)
        ]
        for group in range(turns)
    ]
    for group in copies:
        for piece in group:
            for copy in piece:
                copy.start()

    def turn(group, pair):
        first = group * block + 2 * pair
        stacked = jnp.concatenate(
            [bank[first], bank[half + first], bank[first + 1], bank[half + first + 1]], axis=0
        )
        place = flat.at[group % 2]
        for which in range(2):
            base = (2 * pair + which) * rows
            place[pl.ds(base, margin), :] = zeros
            place[pl.ds(base + margin + taps, margin), :] = zeros
        for part in range(taps // step):
            turned = lax.dot_general(
                eye,
                stacked[:, part * step : (part + 1) * step],
                (((1,), (1,)), ((), ())),
                preferred_element_type=jnp.float32,
            )
            for which in range(2):
                base = (2 * pair + which) * rows + margin + part * step
                place[pl.ds(base, step), :] = turned[:, which * LANES : (which + 1) * LANES]

    pairs = block // 2
    for piece in range(pieces):
        for copy in copies[0][piece]:
            copy.wait()
        for pair in range(piece * size // 2, (piece + 1) * size // 2):
            turn(0, pair)

    for group in range(turns):
        place = flat.at[group % 2]
        start = group * block

        def tap(index):
            value = place[pl.ds(index + margin, block, stride=rows), :]
            return value, pltpu.roll(value, chans, 1)

        def store(ref, tile, early, late):
            ref[tile, start : start + block] = jnp.where(low, early[0], late[1]).astype(jnp.bfloat16)
            ref[tile, half + start : half + start + block] = jnp.where(
                low, early[1], late[0]
            ).astype(jnp.bfloat16)

        if group + 1 < turns:
            for piece in copies[group + 1]:
                for copy in piece:
                    copy.wait()

        early = tap(-4)
        for tile in range(tiles):
            if group + 1 < turns and tile % (tiles // pairs) == 0 and tile // (tiles // pairs) < pairs:
                turn(group + 1, tile // (tiles // pairs))
            middle = tap(2 * tile - 3)
            late = tap(2 * tile - 2)
            store(even_ref, tile, early, middle)
            store(odd_ref, tile, middle, late)
            early = late


def bank_tiles(atom_bank):
    atoms, chans, taps = atom_bank.shape
    tiles = taps // 2 + 4
    rows = taps + 17
    block = 16
    turns = atoms // 2 // block
    shape = jax.ShapeDtypeStruct((tiles, atoms, LANES), jnp.bfloat16)
    spec = pl.BlockSpec(memory_space=pltpu.VMEM)
    return pl.pallas_call(
        functools.partial(bank_kernel, rows),
        in_specs=[pl.BlockSpec(memory_space=pltpu.HBM)],
        out_specs=[spec, spec],
        out_shape=[shape, shape],
        scratch_shapes=[
            pltpu.VMEM(atom_bank.shape, jnp.bfloat16),
            pltpu.VMEM((2, block * rows, LANES), jnp.float32),
            pltpu.SemaphoreType.DMA((turns, 4, 2)),
        ],
        compiler_params=pltpu.CompilerParams(vmem_limit_bytes=24 * 1024 * 1024),
        name="bank_tiles",
    )(pltpu.with_memory_space_constraint(atom_bank, pltpu.HBM))


def turn_kernel(even_ref, odd_ref, even_out, odd_out):
    tiles = even_ref.shape[0]
    rows = even_out.shape[1]
    wide = 2 * LANES
    eye = (
        lax.broadcasted_iota(jnp.int32, (wide, wide), 0)
        == lax.broadcasted_iota(jnp.int32, (wide, wide), 1)
    ).astype(jnp.bfloat16)
    unroll = next(n for n in (260, 52, 20, 4) if tiles % n == 0)

    def loop(turn, carry):
        for inner in range(0, unroll, 4):
            tile = turn * unroll + inner
            stacked = jnp.concatenate(
                [
                    jnp.concatenate([ref[tile + which], ref[tile + 2 + which]], axis=1)
                    for which in range(2)
                    for ref in (odd_ref, even_ref)
                ],
                axis=0,
            )
            turned = lax.dot_general(
                eye, stacked, (((1,), (1,)), ((), ())), preferred_element_type=jnp.float32
            ).astype(jnp.bfloat16)
            for which in range(4):
                part = turned[which // 2 * LANES :, which % 2 * LANES : (which % 2 + 1) * LANES]
                odd_out[tile + which] = part[:rows]
                even_out[tile + which] = part[rows : 2 * rows]
        return carry

    lax.fori_loop(0, tiles // unroll, loop, 0)


def turn_tiles(even, odd):
    tiles = even.shape[0]
    shape = jax.ShapeDtypeStruct((tiles, LANES // 2, LANES), jnp.bfloat16)
    spec = pl.BlockSpec(memory_space=pltpu.VMEM)
    return pl.pallas_call(
        turn_kernel,
        in_specs=[spec, spec],
        out_specs=[spec, spec],
        out_shape=[shape, shape],
        compiler_params=pltpu.CompilerParams(vmem_limit_bytes=VMEM),
        cost_estimate=pl.CostEstimate(
            flops=tiles * LANES**3 * 4, bytes_accessed=4 * even.size * 2, transcendentals=0
        ),
        name="turn_tiles",
    )(even, odd)


def conv_kernel(transposed, edge, own_ref, beside_ref, even, odd, out_ref, base, spread, total):
    run, parts, width = own_ref.shape
    lanes = width // LANES

    beside = beside_ref[...].astype(jnp.float32)
    if edge is not None:
        axis, last = edge
        beside = jnp.where(lax.axis_index(axis) == last, 0.0, beside)
    own_start = 0 if transposed else parts
    base[:, own_start : own_start + parts] = own_ref[...].astype(jnp.float32)
    base[:, parts - own_start : 2 * parts - own_start] = beside

    def fill(shift):
        window = base[:, shift : shift + parts].astype(jnp.bfloat16)
        for lane in range(lanes):
            spread[lane, shift * run : (shift + 1) * run] = window[:, :, lane * LANES : (lane + 1) * LANES]

    def block(step):
        if transposed:
            picks = [(even, 1, 0), (odd, 2, 1), (even, 2, 1), (odd, 3, 2)]
        else:
            picks = [(even, 2, 3), (odd, 1, 2), (even, 1, 2), (odd, 0, 1)]
        return jnp.concatenate(
            [
                jnp.concatenate([ref[2 * step + left], ref[2 * step + right]], axis=1)
                for ref, left, right in picks
            ],
            axis=0,
        )

    def rows(step):
        start = step if transposed else parts * run - step
        return [spread[lane, start : start + run].reshape(run * parts, LANES) for lane in range(lanes)]

    def product(first, count):
        left = jnp.concatenate([part for i in range(count) for part in rows(first + i)], axis=1)
        right = jnp.concatenate([block(first + i) for i in range(count)], axis=0)
        return jnp.dot(left, right, preferred_element_type=jnp.float32)

    order = list(range(parts + 1)) if transposed else list(range(parts, -1, -1))
    fill(order[0])
    total[0] = product(0, 1)
    total[1] = jnp.zeros_like(total[1])
    for turn in range(0, parts, 2):
        fill(order[turn + 1])
        fill(order[turn + 2])
        total[turn // 2 % 2] += product(1 + turn * run, 2 * run)
    out_ref[...] = (total[0] + total[1]).reshape(out_ref.shape).astype(out_ref.dtype)


def convolve(own, beside, tiles, transposed, edge=None):
    run, parts, width = own.shape
    even, odd = tiles
    steps = run * parts + 1
    out_width = PHASES * LANES // 2
    flops = 2 * run * parts * width * out_width * steps
    return pl.pallas_call(
        functools.partial(conv_kernel, transposed, edge),
        in_specs=[pl.BlockSpec(memory_space=pltpu.VMEM)] * 4,
        out_specs=pl.BlockSpec(memory_space=pltpu.VMEM),
        out_shape=jax.ShapeDtypeStruct((run, parts, out_width), jnp.bfloat16),
        scratch_shapes=[
            pltpu.VMEM((run, 2 * parts, width), jnp.float32),
            pltpu.VMEM((width // LANES, (parts + 1) * run, parts, LANES), jnp.bfloat16),
            pltpu.VMEM((2, run * parts, out_width), jnp.float32),
        ],
        compiler_params=pltpu.CompilerParams(vmem_limit_bytes=VMEM),
        cost_estimate=pl.CostEstimate(
            flops=flops, bytes_accessed=even.size * 4 + own.size * 8, transcendentals=0
        ),
        name="correlate" if transposed else "synthesize",
    )(own, beside, even, odd)


def shifted(value, axis, steps):
    count = lax.axis_size(axis)
    if count == 1:
        return jnp.zeros_like(value)
    return lax.ppermute(value, axis, [(i, (i + steps) % count) for i in range(count)])


def partner(value, axis, step):
    return lax.ppermute(value, axis, [(i, i ^ step) for i in range(lax.axis_size(axis))])


def after(value, *others):
    return lax.optimization_barrier((value, *others))[0]


def summed(value, axis, gate=None, early_gate=None):
    step = lax.axis_size(axis) // 2
    first = step
    while step:
        if step > 1:
            value = value.astype(jnp.bfloat16)
        other = partner(value, axis, step)
        if early_gate is not None and step == first:
            other = after(other, early_gate)
        step //= 2
        if gate is not None and not step:
            other = after(other, gate)
        value = value.astype(jnp.float32) + other.astype(jnp.float32)
    return value


def body(signal, codes_init, atom_bank, step_size, threshold):
    atoms, chans, taps = atom_bank.shape
    held = LANES // 2
    if chans < held:
        atom_bank = jnp.pad(atom_bank, ((0, 0), (0, held - chans), (0, 0)))
        signal = jnp.pad(signal, ((0, held - chans), (0, 0)))
    low, high, heard_low, heard_high, step, bound = to_blocks(
        taps, (codes_init, signal), (step_size, threshold)
    )
    tiles = bank_tiles(atom_bank)

    def shrink(current, gradient):
        moved = current - step * gradient
        return moved - jnp.clip(moved, -bound, bound)

    last = lax.axis_size("tm") - 1
    turned = None
    low16, high16 = low.astype(jnp.bfloat16), high.astype(jnp.bfloat16)
    earlier = shifted(high16, "tm", 1)
    for sweep in range(ITERS):
        recon_low = convolve(low16, earlier, tiles, False, ("tm", 0))
        recon_high = convolve(after(high16, recon_low), low16, tiles, False)
        misfit_low = summed(recon_low, "atom") - heard_low
        rounded_low = misfit_low.astype(jnp.bfloat16)
        following = shifted(rounded_low, "tm", -1)
        gate = None
        if turned is None:
            turned = turn_tiles(*(after(tile, rounded_low) for tile in tiles))
            gate = turned[0]
        misfit_high = summed(recon_high, "atom", gate) - heard_high
        rounded_high = misfit_high.astype(jnp.bfloat16)
        if sweep < ITERS - 1:
            gradient_high = convolve(rounded_high, following, turned, True, ("tm", last))
            gradient_low = convolve(after(rounded_low, gradient_high), rounded_high, turned, True)
            high = shrink(high, summed(gradient_high, "chan", None, gradient_low))
            high16 = high.astype(jnp.bfloat16)
            earlier = shifted(high16, "tm", 1)
            low = shrink(low, summed(gradient_low, "chan", None, earlier))
            low16 = low.astype(jnp.bfloat16)
        else:
            gradient_low = convolve(rounded_low, rounded_high, turned, True)
            gradient_high = convolve(rounded_high, following, turned, True, ("tm", last))
            low = shrink(low, summed(gradient_low, "chan"))
            high = shrink(high, summed(gradient_high, "chan"))
    return from_blocks(low, high), from_blocks(misfit_low, misfit_high)[:chans]


def solution(mesh):
    placed = (P("chan", "tm"), P("atom", "tm"), P("atom", "chan", None), P("atom"), P("atom"))
    return jax.shard_map(
        body,
        mesh=mesh,
        in_specs=placed,
        out_specs=(P("atom", "tm"), P("chan", "tm")),
        check_vma=False,
    )
```
